32 devices in a mesh: dp: 8 (over y, x, core), tensor: 4 (over z).
Axes of the slice: x: 2, y: 2, z: 4, core: 2. Of those that a mesh axis runs over, the one named last changes fastest.
Arguments:
- inputs: bfloat16 [16384, 768], P('dp'), may hold values from -6 to 6
- gain1: float32 [768], replicated, may hold values from 0.1 to 1.9
- bias1: float32 [768], replicated, may hold values from -1 to 1
- w_qkv: bfloat16 [768, 3, 768], P(None, None, 'tensor'), may hold values from -0.3125 to 0.3125
- bias_q: float32 [768], P('tensor'), may hold values from -1.5 to 1.5
- bias_v: float32 [768], P('tensor'), may hold values from -1.5 to 1.5
- w_out: bfloat16 [768, 768], P('tensor'), may hold values from -1 to 1
- bias_out: float32 [768], replicated, may hold values from -1 to 1
- gain2: float32 [768], replicated, may hold values from 0.1 to 1.9
- bias2: float32 [768], replicated, may hold values from -1 to 1
- w_fc: bfloat16 [768, 3072], P(None, 'tensor'), may hold values from -0.21875 to 0.21875
- bias_fc: float32 [3072], P('tensor'), may hold values from -1.5 to 1.5
- w_proj: bfloat16 [3072, 768], P('tensor'), may hold values from -0.15625 to 0.15625
- bias_proj: float32 [768], replicated, may hold values from -2 to 2
- cotangent: bfloat16 [16384, 768], P('dp'), may hold values from -6 to 6
Outputs:
- output: bfloat16 [16384, 768], P('dp')
- d_inputs: bfloat16 [16384, 768], P('dp')
- d_gain1: float32 [768], replicated
- d_bias1: float32 [768], replicated
- d_w_qkv: float32 [768, 3, 768], P(None, None, 'tensor')
- d_bias_q: float32 [768], P('tensor')
- d_bias_v: float32 [768], P('tensor')
- d_w_out: float32 [768, 768], P('tensor')
- d_bias_out: float32 [768], replicated
- d_gain2: float32 [768], replicated
- d_bias2: float32 [768], replicated
- d_w_fc: float32 [768, 3072], P(None, 'tensor')
- d_bias_fc: float32 [3072], P('tensor')
- d_w_proj: float32 [3072, 768], P('tensor')
- d_bias_proj: float32 [768], replicated
The draws below stay inside these ranges and needn't reach their ends.
All inputs are finite; a program needn't handle non-finite values.
Results may differ from the reference program's by a relative error of at most 0.02.
Values may be sent and summed in bfloat16 or wider, within the bound.
No kernel may reach another device: no remote copies, remote signals or barrier semaphores. Data moves between devices by JAX's collectives and lax.ppermute only.
A program may use at most 128 MiB of HBM per device.

```python
import jax
import jax.numpy as jnp
from jax import lax

D = 768
HEADS = 12
HEAD = 64
FF = 3072
LEN = 1024
SEQS = 16
TOKENS = 16384
N_TENSOR = 4


def shard_levels(rng, extent, pieces, smallest, largest):
    loudness, own = 1.0, jax.random.fold_in(rng, 6)
    for dim, shards_of in pieces:
        steps = jnp.exp(jax.random.uniform(jax.random.fold_in(own, dim), (shards_of,), jnp.float32, smallest / len(pieces), largest / len(pieces)))
        loudness = loudness * jnp.repeat(steps, extent[dim] // shards_of).reshape([-1 if axis == dim else 1 for axis in range(len(extent))])
    return loudness


def bell_draw(own_key, extent, scale, most, cuts=(), held_as=jnp.bfloat16):
    values = jax.random.normal(own_key, extent, jnp.float32) * scale
    if len(cuts) > 0:
        values = shard_levels(own_key, extent, cuts, -0.22, 0.18) * values
    return jnp.clip(values, min=-most, max=most).astype(held_as)


def setup_inputs(seed: int = 0) -> dict:
    key_of = jax.random.split(jax.random.key(seed), 16)
    return {
        "inputs": bell_draw(key_of[0], (TOKENS, D), 1.0, 6.0, ((0, 8),)),
        "gain1": jnp.clip(1.0 + 0.18 * jax.random.normal(key_of[1], (D,), jnp.float32), 0.1, 1.9),
        "bias1": bell_draw(key_of[2], (D,), 0.2, 1.0, (), jnp.float32),
        "w_qkv": bell_draw(key_of[3], (D, 3, D), (D // 2) ** -0.5, 0.3125, ((2, 4),)),
        "bias_q": bell_draw(key_of[4], (D,), 0.3, 1.5, ((0, 4),), jnp.float32),
        "bias_v": bell_draw(key_of[5], (D,), 0.3, 1.5, ((0, 4),), jnp.float32),
        "w_out": bell_draw(key_of[6], (D, D), (D // 24) ** -0.5, 1.0, ((0, 4),)),
        "bias_out": bell_draw(key_of[7], (D,), 0.2, 1.0, (), jnp.float32),
        "gain2": jnp.clip(1.0 + 0.18 * jax.random.normal(key_of[8], (D,), jnp.float32), 0.1, 1.9),
        "bias2": bell_draw(key_of[9], (D,), 0.2, 1.0, (), jnp.float32),
        "w_fc": bell_draw(key_of[10], (D, FF), D ** -0.5, 0.21875, ((1, 4),)),
        "bias_fc": bell_draw(key_of[11], (FF,), 0.3, 1.5, ((0, 4),), jnp.float32),
        "w_proj": bell_draw(key_of[12], (FF, D), (FF // 2) ** -0.5, 0.15625, ((0, 4),)),
        "bias_proj": bell_draw(key_of[13], (D,), 0.4, 2.0, (), jnp.float32),
        "cotangent": bell_draw(key_of[14], (TOKENS, D), 1.0, 6.0, ((0, 8),)),
    }


@jax.custom_vjp
def low(v):
    return lax.optimization_barrier(v.astype(jnp.bfloat16)).astype(jnp.float32)

@jax.custom_vjp
def low_back(v):
    return v

def low_keep(v):
    return (low(v), None)

def low_pass(kept, grad):
    return (grad,)

def back_keep(v):
    return (v, None)

def back_low(kept, grad):
    return (low(grad),)
low.defvjp(low_keep, low_pass)
low_back.defvjp(back_keep, back_low)
HIGH = lax.Precision.HIGHEST

def layer_norm(value, gain, shift):
    centre = value - lax.optimization_barrier(jnp.mean(value, axis=-1, keepdims=True))
    spread = lax.optimization_barrier(jnp.mean(centre * centre, axis=-1, keepdims=True))
    return centre * lax.rsqrt(spread + 1e-05) * gain + shift

def gelu(value):
    return 0.5 * value * (1.0 + jnp.tanh(0.7978845608028654 * (value + 0.044715 * value * value * value)))

def attend_one(block):
    query, keys, values = block
    scores = jnp.einsum('qhe,khe->hqk', query, keys, precision=HIGH)
    scores = low_back(scores)
    rows = lax.broadcasted_iota(jnp.int32, (LEN, LEN), 0)
    cols = lax.broadcasted_iota(jnp.int32, (LEN, LEN), 1)
    scores = jnp.where((cols <= rows)[None], scores, -1e+30)
    top = lax.optimization_barrier(jnp.max(scores, axis=-1, keepdims=True))
    expo = jnp.exp(scores - top)
    probs = expo / lax.optimization_barrier(jnp.sum(expo, axis=-1, keepdims=True))
    probs = low(probs)
    return jnp.einsum('hqk,khe->qhe', probs, values, precision=HIGH)

def forward(x, gain1, bias1, w_qkv, bias_q, bias_v, w_out, bias_out, gain2, bias2, w_fc, bias_fc, w_proj, bias_proj):
    groups = N_TENSOR
    local = D // groups
    hidden = FF // groups
    count = x.shape[0]
    scale = HEAD ** (-0.5)
    a1 = low(layer_norm(x, gain1, bias1))
    a1g = low_back(jnp.broadcast_to(a1, (groups,) + a1.shape))
    proj = jnp.einsum('gtd,dcge->gtce', a1g, w_qkv.reshape(D, 3, groups, local), precision=HIGH)
    query = (proj[:, :, 0] + bias_q.reshape(groups, 1, local)) * scale
    keys = proj[:, :, 1]
    values = proj[:, :, 2] + bias_v.reshape(groups, 1, local)

    def heads(value):
        value = low(low_back(value))
        return value.transpose(1, 0, 2).reshape(SEQS, LEN, HEADS, HEAD)
    attn = lax.map(jax.checkpoint(attend_one), (heads(query), heads(keys), heads(values)))
    attn = low(low_back(attn.reshape(count, groups, local)))
    parts = jnp.einsum('tge,ged->gtd', attn, w_out.reshape(groups, local, D), precision=HIGH)
    parts = low(low_back(parts))
    h = x + lax.optimization_barrier(jnp.sum(parts, axis=0)) + bias_out
    a2 = low(layer_norm(h, gain2, bias2))
    a2g = low_back(jnp.broadcast_to(a2, (groups,) + a2.shape))
    upper = jnp.einsum('gtd,dgf->gtf', a2g, w_fc.reshape(D, groups, hidden), precision=HIGH)
    upper = low_back(upper + bias_fc.reshape(groups, 1, hidden))
    active = low(gelu(upper))
    parts2 = jnp.einsum('gtf,gfd->gtd', active, w_proj.reshape(groups, hidden, D), precision=HIGH)
    parts2 = low(low_back(parts2))
    return h + lax.optimization_barrier(jnp.sum(parts2, axis=0)) + bias_proj

def reference(inputs, gain1, bias1, w_qkv, bias_q, bias_v, w_out, bias_out, gain2, bias2, w_fc, bias_fc, w_proj, bias_proj, cotangent):
    params = (inputs, gain1, bias1, w_qkv, bias_q, bias_v, w_out, bias_out, gain2, bias2, w_fc, bias_fc, w_proj, bias_proj)
    params = tuple((p.astype(jnp.float32) for p in params))
    result, pull = jax.vjp(forward, *params)
    grads = pull(cotangent.astype(jnp.float32))
    return (result.astype(jnp.bfloat16), grads[0].astype(jnp.bfloat16), grads[1], grads[2], grads[3], grads[4], grads[5], grads[6], grads[7], grads[8], grads[9], grads[10], grads[11], grads[12], grads[13])
```

```python
import jax
import jax.numpy as jnp
import numpy as np
from jax import lax
from jax.experimental import pallas as pl
from jax.experimental.pallas import tpu as pltpu
from jax.sharding import PartitionSpec as P

HEAD = 64
LEN = 1024
BLOCK = 256
VMEM = 32 * 2**20
LOW = jnp.bfloat16
WIDE = jnp.float32

NN = (((1,), (0,)), ((), ()))
NT = (((1,), (1,)), ((), ()))
TN = (((0,), (0,)), ((), ()))
TT = (((0,), (1,)), ((), ()))


def dot(left, right, dims=NN):
    return lax.dot_general(left, right, dims, preferred_element_type=WIDE)


def gelu(value):
    return (
        0.5
        * value
        * (1.0 + jnp.tanh(0.7978845608028654 * (value + 0.044715 * value * value * value)))
    )


def norm_parts(value):
    centre = value - jnp.mean(value, axis=-1, keepdims=True)
    rstd = lax.rsqrt(jnp.mean(centre * centre, axis=-1, keepdims=True) + 1e-05)
    return (centre * rstd, rstd)


def norm_back(normed, rstd, gain, grad):
    scaled = grad * gain
    inner = (
        scaled
        - jnp.mean(scaled, axis=-1, keepdims=True)
        - normed * jnp.mean(scaled * normed, axis=-1, keepdims=True)
    )
    return (rstd * inner, jnp.sum(grad * normed, axis=0), jnp.sum(grad, axis=0))


def causal(scores):
    keys = lax.broadcasted_iota(jnp.int32, scores.shape, 0)
    queries = lax.broadcasted_iota(jnp.int32, scores.shape, 1)
    return keys <= queries


def attend(q_ref, k_ref, v_ref, o_ref, lse_ref):
    query, values = q_ref[0, 0], v_ref[0, 0]
    keys = k_ref[0, 0].T
    for lo in range(0, LEN, BLOCK):
        hi = lo + BLOCK
        near = dot(keys[lo:hi], query[:, lo:hi])
        near = jnp.where(causal(near), near, -1e30)
        top = jnp.max(near, axis=0, keepdims=True)
        if lo:
            far = dot(keys[:lo], query[:, lo:hi])
            top = jnp.maximum(top, jnp.max(far, axis=0, keepdims=True))
        near = jnp.exp(near - top)
        total = jnp.sum(near, axis=0, keepdims=True)
        out = dot(values[:, lo:hi], near.astype(LOW))
        if lo:
            far = jnp.exp(far - top)
            total += jnp.sum(far, axis=0, keepdims=True)
            out += dot(values[:, :lo], far.astype(LOW))
        o_ref[0, :, lo:hi] = (out / total).astype(LOW)
        lse_ref[0, :, lo:hi] = top + jnp.log(total)


def attend_back(q_ref, k_ref, v_ref, o_ref, do_ref, lse_ref, out_ref, dq_ref):
    query, keys_t, d_out = q_ref[0, 0], k_ref[0, 0], do_ref[0]
    keys, values = keys_t.T, v_ref[0, 0].T
    lse = lse_ref[0]
    delta = jnp.sum(d_out.astype(WIDE) * o_ref[0].astype(WIDE), axis=0, keepdims=True)

    def part(lo, hi, begin, end, mask):
        probs = jnp.exp(dot(keys[lo:hi], query[:, begin:end]) - lse[:, begin:end])
        if mask:
            probs = jnp.where(causal(probs), probs, 0.0)
        d_probs = dot(values[lo:hi], d_out[:, begin:end])
        d_scores = (probs * (d_probs - delta[:, begin:end])).astype(LOW)
        d_values = dot(d_out[:, begin:end], probs.astype(LOW), NT)
        d_keys = dot(query[:, begin:end], d_scores, NT)
        d_query = dot(keys_t[:, lo:hi], d_scores)
        if lo == 0:
            dq_ref[:, begin:end] = d_query
        else:
            dq_ref[:, begin:end] += d_query
        return d_keys, d_values

    for lo in range(0, LEN, BLOCK):
        hi = lo + BLOCK
        d_keys, d_values = part(lo, hi, lo, hi, True)
        if hi < LEN:
            more_keys, more_values = part(lo, hi, hi, LEN, False)
            d_keys += more_keys
            d_values += more_values
        out_ref[1, 0, :, lo:hi] = d_keys.astype(LOW)
        out_ref[2, 0, :, lo:hi] = d_values.astype(LOW)
    d_query = dq_ref[...].astype(LOW).astype(WIDE) * HEAD ** (-0.5)
    out_ref[0, 0] = d_query.astype(LOW)


def kind(which):
    return pl.BlockSpec((1, 1, HEAD, LEN), lambda head: (which, head, 0, 0))


QKV = [kind(0), kind(1), kind(2)]
PER_HEAD = pl.BlockSpec((1, HEAD, LEN), lambda head: (head, 0, 0))
PER_ROW = pl.BlockSpec((1, 1, LEN), lambda head: (head, 0, 0))


def attention(qkv):
    heads = qkv.shape[1]
    return pl.pallas_call(
        attend,
        grid=(heads,),
        in_specs=QKV,
        out_specs=[PER_HEAD, PER_ROW],
        out_shape=[
            jax.ShapeDtypeStruct((heads, HEAD, LEN), LOW),
            jax.ShapeDtypeStruct((heads, 1, LEN), WIDE),
        ],
        compiler_params=pltpu.CompilerParams(vmem_limit_bytes=VMEM),
        cost_estimate=pl.CostEstimate(
            flops=heads * 8 * HEAD * LEN * LEN,
            bytes_accessed=heads * LEN * HEAD * 8,
            transcendentals=heads * LEN * LEN,
        ),
        name="attention",
    )(qkv, qkv, qkv)


def attention_back(qkv, out, d_out, lse):
    heads = qkv.shape[1]
    return pl.pallas_call(
        attend_back,
        grid=(heads,),
        in_specs=QKV + [PER_HEAD, PER_HEAD, PER_ROW],
        out_specs=pl.BlockSpec((3, 1, HEAD, LEN), lambda head: (0, head, 0, 0)),
        out_shape=jax.ShapeDtypeStruct((3, heads, HEAD, LEN), LOW),
        scratch_shapes=[pltpu.VMEM((HEAD, LEN), WIDE)],
        compiler_params=pltpu.CompilerParams(vmem_limit_bytes=VMEM),
        cost_estimate=pl.CostEstimate(
            flops=heads * 20 * HEAD * LEN * LEN,
            bytes_accessed=heads * LEN * HEAD * 16,
            transcendentals=heads * LEN * LEN,
        ),
        name="attention_back",
    )(qkv, qkv, qkv, out, d_out, lse)


def bits(size, odd):
    above = [1 << b for b in range(1, size.bit_length() - 1)]
    return above if odd else above[::-1]


def exchanges(size):
    steps = [
        [(d, d ^ (odd if d & 1 else even)) for d in range(size)]
        for even, odd in zip(bits(size, False), bits(size, True))
    ]
    return steps + ([[(d, d ^ 1) for d in range(size)]] if size > 1 else [])


def slot_masks(size, odd):
    def above(parity):
        held = [0]
        for bit in bits(size, parity):
            held = held + [m ^ bit for m in held]
        return held

    return above(odd) + ([1 ^ m for m in above(not odd)] if size > 1 else [])


def gather_plane(piece, size):
    held = piece[None]
    for step in exchanges(size):
        held = jnp.concatenate([held, lax.ppermute(held, "dp", step)], axis=0)
    return held


def sum_plane(held, size):
    for step in exchanges(size)[::-1]:
        half = held.shape[0] // 2
        taken = lax.ppermute(held[half:], "dp", step)
        held = (held[:half].astype(WIDE) + taken.astype(WIDE)).astype(LOW)
    return held[0]


def across(piece, mask, size):
    return lax.ppermute(piece, "tensor", [(t, t ^ mask) for t in range(size)])


ORDER = (0, 2, 1, 3)


def gather_tensor(piece, size):
    return jnp.stack([piece] + [across(piece, m, size) for m in ORDER[1:]])


def sum_tensor(held, size):
    total = held[0].astype(WIDE)
    for at, mask in enumerate(ORDER[1:], 1):
        total += across(held[at], mask, size).astype(WIDE)
    return total


def ring_tensor(piece, size):
    me = lax.axis_index("tensor")
    rows = piece.shape[0]
    whole = jnp.zeros((size * rows,) + piece.shape[1:], piece.dtype)
    for step in range(size):
        if step:
            piece = lax.ppermute(piece, "tensor", [(t, (t + 1) % size) for t in range(size)])
        at = lax.rem(me - step + size, size) * rows
        whole = lax.dynamic_update_slice(whole, piece, (at, 0))
    return whole


def pick(order_ref, in_ref, out_ref):
    out_ref[...] = in_ref[...].astype(out_ref.dtype)


def reorder(slots, order, dtype):
    count, rows, width = slots.shape
    return pl.pallas_call(
        pick,
        grid_spec=pltpu.PrefetchScalarGridSpec(
            num_scalar_prefetch=1,
            grid=(count,),
            in_specs=[pl.BlockSpec((1, rows, width), lambda j, order: (order[j], 0, 0))],
            out_specs=pl.BlockSpec((1, rows, width), lambda j, order: (j, 0, 0)),
        ),
        out_shape=jax.ShapeDtypeStruct(slots.shape, dtype),
        compiler_params=pltpu.CompilerParams(vmem_limit_bytes=VMEM),
        name="reorder",
    )(order, slots)


def shards(
    inputs,
    gain1,
    bias1,
    w_qkv,
    bias_q,
    bias_v,
    w_out,
    bias_out,
    gain2,
    bias2,
    w_fc,
    bias_fc,
    w_proj,
    bias_proj,
    cotangent,
):
    n_dp, n_t = lax.axis_size("dp"), lax.axis_size("tensor")
    place, me = lax.axis_index("dp"), lax.axis_index("tensor")
    count, width = inputs.shape
    local = w_qkv.shape[2]
    hidden = w_fc.shape[1]
    heads = local // HEAD
    scale = HEAD ** (-0.5)
    own = count // n_t
    half = lax.rem(me, 2)
    slots = place ^ jnp.where(
        lax.rem(place, 2) == 1,
        np.array(slot_masks(n_dp, True), np.int32),
        np.array(slot_masks(n_dp, False), np.int32),
    )
    index = jnp.arange(n_dp, dtype=jnp.int32)
    where = jnp.sum(jnp.where(slots[None, :] == index[:, None], index[None, :], 0), axis=1)

    qkv_own = w_qkv.reshape(width, 3 * local)
    rows_q, rows_o, rows_f = width // n_dp, local // n_dp, hidden // n_dp
    piece = lax.dynamic_slice_in_dim(qkv_own, place * rows_q, rows_q, 0)
    piece = gather_plane(across(piece, 2, n_t), n_dp)
    qkv_other = reorder(piece, where, LOW).reshape(width, 3 * local)
    bias_own = jnp.stack([bias_q, jnp.zeros_like(bias_q), bias_v])
    bias_other = across(bias_own, 2, n_t)
    piece = lax.dynamic_slice_in_dim(w_out, place * rows_o, rows_o, 0)
    piece = gather_plane(gather_tensor(piece, n_t), n_dp)
    w_out_all = jnp.take(piece, where, axis=0).transpose(1, 0, 2, 3).reshape(n_t * local, width)
    piece = lax.dynamic_slice_in_dim(w_fc, place * rows_f, rows_f, 1).T
    w_fc_all = gather_plane(gather_tensor(piece, n_t), n_dp).reshape(n_t * hidden, width)
    piece = lax.dynamic_slice_in_dim(w_proj, place * rows_f, rows_f, 0)
    w_proj_all = gather_plane(gather_tensor(piece, n_t), n_dp).reshape(n_t * hidden, width)
    groups = jnp.stack([me ^ m for m in ORDER])
    bias_fc_all = lax.all_gather(bias_fc, "tensor").reshape(n_t, n_dp, rows_f)
    bias_fc_all = bias_fc_all[groups[None, :], slots[:, None]].reshape(n_t * hidden)

    x_seq = lax.dynamic_slice_in_dim(inputs, (me // 2) * LEN, LEN, 0).astype(WIDE)
    normed, _ = norm_parts(x_seq)
    a_first = (normed * gain1 + bias1).astype(LOW)

    def project(weight, bias):
        proj = dot(weight, a_first, TT).reshape(3, local, LEN) + bias[:, :, None]
        proj = proj * jnp.array([scale, 1.0, 1.0], WIDE)[:, None, None]
        return proj.astype(LOW).reshape(3, heads, HEAD, LEN)

    def halves(value):
        mine = lax.dynamic_slice_in_dim(value, half * own, own, value.ndim - 1)
        theirs = lax.dynamic_slice_in_dim(value, (1 - half) * own, own, value.ndim - 1)
        return mine, theirs

    proj_a = project(qkv_own, bias_own)
    out_a, lse_a = attention(proj_a)
    mine_a, theirs_a = halves(out_a.reshape(local, LEN))
    theirs_a = across(theirs_a, 1, n_t)
    proj_b = project(qkv_other, bias_other)
    out_b, lse_b = attention(proj_b)
    mine_b, theirs_b = halves(out_b.reshape(local, LEN))
    theirs_b = across(theirs_b, 1, n_t)
    attn_low = jnp.concatenate([mine_a, mine_b, theirs_a, theirs_b], axis=0)

    x_own = lax.dynamic_slice_in_dim(inputs, me * own, own, 0).astype(WIDE)
    dy = lax.dynamic_slice_in_dim(cotangent, me * own, own, 0)
    resid = x_own + dot(attn_low, w_out_all, TN) + bias_out
    normed2, rstd2 = norm_parts(resid)
    a_second = (normed2 * gain2 + bias2).astype(LOW)
    upper = dot(a_second, w_fc_all, NT) + bias_fc_all
    active = gelu(upper).astype(LOW)
    output = (resid + dot(active, w_proj_all) + bias_proj).astype(LOW)
    d_active = dot(dy, w_proj_all, NT)
    d_upper = jax.vjp(gelu, upper)[1](d_active)[0].astype(LOW)
    d_second = dot(d_upper, w_fc_all)
    d_resid_norm, d_gain2, d_bias2 = norm_back(normed2, rstd2, gain2, d_second)
    d_resid = dy.astype(WIDE) + d_resid_norm
    d_resid_low = d_resid.astype(LOW)
    d_attn = dot(w_out_all, d_resid_low, NT).astype(LOW)
    d_mine, d_theirs = d_attn[: 2 * local], d_attn[2 * local :]
    d_theirs = across(d_theirs, 1, n_t)
    d_out = jnp.where(
        half == 0,
        jnp.concatenate([d_mine, d_theirs], axis=1),
        jnp.concatenate([d_theirs, d_mine], axis=1),
    ).reshape(2, heads, HEAD, LEN)

    def reduce_hidden(grad):
        held = sum_plane(grad.astype(LOW).reshape(n_dp, n_t, rows_f, width), n_dp)
        total = sum_tensor(held, n_t).astype(LOW)
        return reorder(gather_plane(total, n_dp), where, WIDE).reshape(hidden, width)

    d_w_proj = reduce_hidden(dot(active, dy, TN))
    d_w_fc = reduce_hidden(dot(d_upper, a_second, TN)).T
    grad = dot(attn_low, d_resid_low).astype(LOW).reshape(n_t, n_dp, rows_o, width)
    grad = jnp.take(grad, slots, axis=1).transpose(1, 0, 2, 3)
    total = sum_tensor(sum_plane(grad, n_dp), n_t).astype(LOW)
    d_w_out = jnp.take(gather_plane(total, n_dp), where, axis=0).astype(WIDE).reshape(local, width)

    d_proj_a = attention_back(proj_a, out_a, d_out[0], lse_a).reshape(3 * local, LEN)
    d_proj_b = attention_back(proj_b, out_b, d_out[1], lse_b).reshape(3 * local, LEN)

    def d_first_of(begin):
        rows_a = lax.dynamic_slice_in_dim(d_proj_a, begin, own, 1)
        rows_b = lax.dynamic_slice_in_dim(d_proj_b, begin, own, 1)
        return dot(rows_a, qkv_own, TT) + dot(rows_b, qkv_other, TT)

    d_theirs = across(d_first_of((1 - half) * own).astype(LOW), 1, n_t)
    d_first = d_first_of(half * own) + d_theirs.astype(WIDE)
    normed1, rstd1 = norm_parts(x_own)
    d_in_norm, d_gain1, d_bias1 = norm_back(normed1, rstd1, gain1, d_first)
    d_inputs = (d_resid + d_in_norm).astype(LOW)

    def by_rows(d_proj):
        return dot(a_first, d_proj, TT).reshape(n_dp, rows_q, 3 * local)

    grad = jnp.stack([by_rows(d_proj_a), by_rows(d_proj_b)], axis=1)
    grad = reorder(grad.reshape(n_dp, 2 * rows_q, 3 * local), slots, LOW)
    total = sum_plane(grad, n_dp)
    total = total[:rows_q].astype(WIDE) + across(total[rows_q:], 2, n_t).astype(WIDE)
    d_w_qkv = reorder(gather_plane(total.astype(LOW), n_dp), where, WIDE)
    d_w_qkv = d_w_qkv.reshape(width, 3, local)

    sums_a = jnp.sum(d_proj_a.reshape(3, local, LEN).astype(WIDE), axis=2)
    sums_b = jnp.sum(d_proj_b.reshape(3, local, LEN).astype(WIDE), axis=2)
    bias_rows = jnp.zeros((3, n_t * local), WIDE)
    bias_rows = lax.dynamic_update_slice(bias_rows, sums_a, (0, me * local))
    bias_rows = lax.dynamic_update_slice(bias_rows, sums_b, (0, (me ^ 2) * local))
    sums_fc = jnp.sum(d_upper.astype(WIDE), axis=0).reshape(n_dp, n_t, rows_f)
    back = jnp.stack([me ^ m for m in range(n_t)])
    back = jnp.array([ORDER.index(m) for m in range(n_t)], jnp.int32)[back]
    sums_fc = sums_fc[where[None, :], back[:, None]].reshape(n_t * hidden // width, width)
    vectors = jnp.concatenate(
        [
            jnp.stack(
                [
                    d_gain1,
                    d_bias1,
                    d_gain2,
                    d_bias2,
                    jnp.sum(d_resid, axis=0),
                    jnp.sum(dy.astype(WIDE), axis=0),
                ]
            ),
            bias_rows,
            sums_fc,
        ],
        axis=0,
    )
    for mask in (1, 2):
        vectors = vectors + across(vectors, mask, n_t)
    for step in exchanges(n_dp):
        vectors = vectors + lax.ppermute(vectors, "dp", step)
    d_gain1, d_bias1, d_gain2, d_bias2, d_bias_out, d_bias_proj = (vectors[r] for r in range(6))
    d_bias_q = lax.dynamic_slice_in_dim(vectors[6], me * local, local, 0)
    d_bias_v = lax.dynamic_slice_in_dim(vectors[8], me * local, local, 0)
    d_bias_fc = lax.dynamic_slice_in_dim(vectors[9:].reshape(-1), me * hidden, hidden, 0)
    return (
        ring_tensor(output, n_t),
        ring_tensor(d_inputs, n_t),
        d_gain1,
        d_bias1,
        d_w_qkv,
        d_bias_q,
        d_bias_v,
        d_w_out,
        d_bias_out,
        d_gain2,
        d_bias2,
        d_w_fc,
        d_bias_fc,
        d_w_proj,
        d_bias_proj,
    )


def solution(mesh):
    placed = (
        P("dp", None),
        P(),
        P(),
        P(None, None, "tensor"),
        P("tensor"),
        P("tensor"),
        P("tensor", None),
        P(),
        P(),
        P(),
        P(None, "tensor"),
        P("tensor"),
        P("tensor", None),
        P(),
        P("dp", None),
    )
    return jax.shard_map(
        shards,
        mesh=mesh,
        in_specs=placed,
        out_specs=(
            P("dp", None),
            P("dp", None),
            P(),
            P(),
            P(None, None, "tensor"),
            P("tensor"),
            P("tensor"),
            P("tensor", None),
            P(),
            P(),
            P(),
            P(None, "tensor"),
            P("tensor"),
            P("tensor", None),
            P(),
        ),
        check_vma=False,
    )
```

```python
import jax
import jax.numpy as jnp
from jax import lax
from jax.experimental import pallas as pl
from jax.experimental.pallas import tpu as pltpu
from jax.sharding import PartitionSpec as P

HEAD = 64
LEN = 1024
BLOCK = 256
VMEM = 32 * 2**20
LOW = jnp.bfloat16
WIDE = jnp.float32

NN = (((1,), (0,)), ((), ()))
NT = (((1,), (1,)), ((), ()))
TN = (((0,), (0,)), ((), ()))
TT = (((0,), (1,)), ((), ()))


def dot(left, right, dims=NN):
    return lax.dot_general(left, right, dims, preferred_element_type=WIDE)


def norm_parts(value):
    centre = value - jnp.mean(value, axis=-1, keepdims=True)
    rstd = lax.rsqrt(jnp.mean(centre * centre, axis=-1, keepdims=True) + 1e-05)
    return (centre * rstd, rstd)


def norm_back(normed, rstd, gain, grad):
    scaled = grad * gain
    inner = (
        scaled
        - jnp.mean(scaled, axis=-1, keepdims=True)
        - normed * jnp.mean(scaled * normed, axis=-1, keepdims=True)
    )
    return (rstd * inner, jnp.sum(grad * normed, axis=0), jnp.sum(grad, axis=0))


def causal(scores):
    keys = lax.broadcasted_iota(jnp.int32, scores.shape, 0)
    queries = lax.broadcasted_iota(jnp.int32, scores.shape, 1)
    return keys <= queries


def attend(q_ref, k_ref, v_ref, o_ref, lse_ref):
    query, values = q_ref[0, 0], v_ref[0, 0]
    keys = k_ref[0, 0].T
    for lo in range(0, LEN, BLOCK):
        hi = lo + BLOCK
        near = dot(keys[lo:hi], query[:, lo:hi])
        near = jnp.where(causal(near), near, -1e30)
        top = jnp.max(near, axis=0, keepdims=True)
        if lo:
            far = dot(keys[:lo], query[:, lo:hi])
            top = jnp.maximum(top, jnp.max(far, axis=0, keepdims=True))
        near = jnp.exp(near - top)
        total = jnp.sum(near, axis=0, keepdims=True)
        out = dot(values[:, lo:hi], near.astype(LOW))
        if lo:
            far = jnp.exp(far - top)
            total += jnp.sum(far, axis=0, keepdims=True)
            out += dot(values[:, :lo], far.astype(LOW))
        o_ref[0, :, lo:hi] = (out / total).astype(LOW)
        lse_ref[0, :, lo:hi] = top + jnp.log(total)


def attend_back(q_ref, k_ref, v_ref, o_ref, do_ref, lse_ref, out_ref, dq_ref):
    query, keys_t, d_out = q_ref[0, 0], k_ref[0, 0], do_ref[0]
    keys, values = keys_t.T, v_ref[0, 0].T
    lse = lse_ref[0]
    delta = jnp.sum(d_out.astype(WIDE) * o_ref[0].astype(WIDE), axis=0, keepdims=True)

    def part(lo, hi, begin, end, mask):
        probs = jnp.exp(dot(keys[lo:hi], query[:, begin:end]) - lse[:, begin:end])
        if mask:
            probs = jnp.where(causal(probs), probs, 0.0)
        d_probs = dot(values[lo:hi], d_out[:, begin:end])
        d_scores = (probs * (d_probs - delta[:, begin:end])).astype(LOW)
        d_values = dot(d_out[:, begin:end], probs.astype(LOW), NT)
        d_keys = dot(query[:, begin:end], d_scores, NT)
        d_query = dot(keys_t[:, lo:hi], d_scores)
        if lo == 0:
            dq_ref[:, begin:end] = d_query
        else:
            dq_ref[:, begin:end] += d_query
        return d_keys, d_values

    for lo in range(0, LEN, BLOCK):
        hi = lo + BLOCK
        d_keys, d_values = part(lo, hi, lo, hi, True)
        if hi < LEN:
            more_keys, more_values = part(lo, hi, hi, LEN, False)
            d_keys += more_keys
            d_values += more_values
        out_ref[1, 0, :, lo:hi] = d_keys.astype(LOW)
        out_ref[2, 0, :, lo:hi] = d_values.astype(LOW)
    d_query = dq_ref[...].astype(LOW).astype(WIDE) * HEAD ** (-0.5)
    out_ref[0, 0] = d_query.astype(LOW)


def kind(which):
    return pl.BlockSpec((1, 1, HEAD, LEN), lambda head: (which, head, 0, 0))


QKV = [kind(0), kind(1), kind(2)]
PER_HEAD = pl.BlockSpec((1, HEAD, LEN), lambda head: (head, 0, 0))
PER_ROW = pl.BlockSpec((1, 1, LEN), lambda head: (head, 0, 0))


def attention(qkv):
    heads = qkv.shape[1]
    return pl.pallas_call(
        attend,
        grid=(heads,),
        in_specs=QKV,
        out_specs=[PER_HEAD, PER_ROW],
        out_shape=[
            jax.ShapeDtypeStruct((heads, HEAD, LEN), LOW),
            jax.ShapeDtypeStruct((heads, 1, LEN), WIDE),
        ],
        compiler_params=pltpu.CompilerParams(vmem_limit_bytes=VMEM),
        cost_estimate=pl.CostEstimate(
            flops=heads * 8 * HEAD * LEN * LEN,
            bytes_accessed=heads * LEN * HEAD * 8,
            transcendentals=heads * LEN * LEN,
        ),
        name="attention",
    )(qkv, qkv, qkv)


def attention_back(qkv, out, d_out, lse):
    heads = qkv.shape[1]
    return pl.pallas_call(
        attend_back,
        grid=(heads,),
        in_specs=QKV + [PER_HEAD, PER_HEAD, PER_ROW],
        out_specs=pl.BlockSpec((3, 1, HEAD, LEN), lambda head: (0, head, 0, 0)),
        out_shape=jax.ShapeDtypeStruct((3, heads, HEAD, LEN), LOW),
        scratch_shapes=[pltpu.VMEM((HEAD, LEN), WIDE)],
        compiler_params=pltpu.CompilerParams(vmem_limit_bytes=VMEM),
        cost_estimate=pl.CostEstimate(
            flops=heads * 20 * HEAD * LEN * LEN,
            bytes_accessed=heads * LEN * HEAD * 16,
            transcendentals=heads * LEN * LEN,
        ),
        name="attention_back",
    )(qkv, qkv, qkv, out, d_out, lse)


def bits(size, odd):
    above = [1 << b for b in range(1, size.bit_length() - 1)]
    return above if odd else above[::-1]


def exchanges(size):
    steps = [
        [(d, d ^ (odd if d & 1 else even)) for d in range(size)]
        for even, odd in zip(bits(size, False), bits(size, True))
    ]
    return steps + [[(d, d ^ 1) for d in range(size)]]


def turned(value, size, odd):
    count = size.bit_length() - 2
    back = value * 0
    for b in range(count):
        back = back | (((value >> b) & 1) << (count - 1 - b))
    return jnp.where(odd == 1, value, back)


def slot_of(index, place, size):
    mask = index ^ place
    low = mask & 1
    return low * (size // 2) + turned(mask >> 1, size, (place & 1) ^ low)


def index_of(slot, place, size):
    low = slot // (size // 2)
    return ((turned(slot % (size // 2), size, (place & 1) ^ low) << 1) | low) ^ place


def swap(value, step):
    return lax.ppermute(value, "dp", step)


def gather_near(piece, size):
    held = piece[None]
    for step in exchanges(size)[:-1]:
        held = jnp.concatenate([held, swap(held, step)], axis=0)
    return held


def gather_plane(piece, size):
    held = gather_near(piece, size)
    return jnp.concatenate([held, swap(held, exchanges(size)[-1])], axis=0)


def add_low(left, right):
    return (left.astype(WIDE) + right.astype(WIDE)).astype(LOW)


def sum_plane(mine, theirs, size):
    held = add_low(mine, swap(theirs, exchanges(size)[-1]))
    for step in exchanges(size)[-2::-1]:
        half = held.shape[0] // 2
        held = add_low(held[:half], swap(held[half:], step))
    return held[0]


def across(piece, mask, size):
    return lax.ppermute(piece, "tensor", [(t, t ^ mask) for t in range(size)])


ORDER = (0, 2, 1, 3)


def gather_tensor(piece, size):
    return jnp.stack([piece] + [across(piece, m, size) for m in ORDER[1:]])


def sum_tensor(held, size):
    total = held[0].astype(WIDE)
    for at, mask in enumerate(ORDER[1:], 1):
        total += across(held[at], mask, size).astype(WIDE)
    return total.astype(LOW)


def assemble(me_ref, *refs):
    for step, piece_ref in enumerate(refs[:-1]):

        @pl.when(pl.program_id(0) == step)
        def _(piece_ref=piece_ref):
            refs[-1][...] = piece_ref[...]


def ring_tensor(piece, size):
    rows, width = piece.shape
    pieces = [piece]
    for _ in range(size - 1):
        piece = lax.ppermute(piece, "tensor", [(t, (t + 1) % size) for t in range(size)])
        pieces.append(piece)
    return pl.pallas_call(
        assemble,
        grid_spec=pltpu.PrefetchScalarGridSpec(
            num_scalar_prefetch=1,
            grid=(size,),
            in_specs=[pl.BlockSpec((rows, width), lambda g, me: (0, 0))] * size,
            out_specs=pl.BlockSpec(
                (rows, width), lambda g, me: (lax.rem(me[0] - g + size, size), 0)
            ),
        ),
        out_shape=jax.ShapeDtypeStruct((size * rows, width), piece.dtype),
        compiler_params=pltpu.CompilerParams(vmem_limit_bytes=VMEM),
        name="assemble",
    )(lax.axis_index("tensor")[None], *pieces)


def pick(place_ref, *refs):
    for at, in_ref in enumerate(refs[:-1]):
        value = in_ref[...]
        refs[-1][...] = value.reshape(refs[-1].shape).astype(refs[-1].dtype)


def pick_two(place_ref, first_ref, second_ref, out_ref):
    out_ref[0, 0] = first_ref[0].astype(out_ref.dtype)
    out_ref[0, 1] = second_ref[0].astype(out_ref.dtype)


def reorder_call(kernel, place, values, count, in_spec, out_spec, shape, dtype):
    return pl.pallas_call(
        kernel,
        grid_spec=pltpu.PrefetchScalarGridSpec(
            num_scalar_prefetch=1,
            grid=(count,),
            in_specs=[in_spec] * len(values),
            out_specs=out_spec,
        ),
        out_shape=jax.ShapeDtypeStruct(shape, dtype),
        compiler_params=pltpu.CompilerParams(vmem_limit_bytes=VMEM),
        name="reorder",
    )(place[None], *values)


def by_index(slots, place, dtype):
    count, rows, width = slots.shape
    return reorder_call(
        pick,
        place,
        [slots],
        count,
        pl.BlockSpec((1, rows, width), lambda j, p: (slot_of(j, p[0], count), 0, 0)),
        pl.BlockSpec((1, rows, width), lambda j, p: (j, 0, 0)),
        slots.shape,
        dtype,
    )


def by_slot_two(first, second, place):
    count, rows, width = first.shape
    return reorder_call(
        pick_two,
        place,
        [first, second],
        count,
        pl.BlockSpec((1, rows, width), lambda k, p: (index_of(k, p[0], count), 0, 0)),
        pl.BlockSpec((1, 2, rows, width), lambda k, p: (k, 0, 0, 0)),
        (count, 2, rows, width),
        LOW,
    )


def groups_by_index(slots, place):
    count, groups, rows, width = slots.shape
    return reorder_call(
        pick,
        place,
        [slots],
        count,
        pl.BlockSpec((1, groups, rows, width), lambda j, p: (slot_of(j, p[0], count), 0, 0, 0)),
        pl.BlockSpec((groups, 1, rows, width), lambda j, p: (0, j, 0, 0)),
        (groups, count, rows, width),
        LOW,
    )


def groups_by_slot(values, place):
    groups, count, rows, width = values.shape
    return reorder_call(
        pick,
        place,
        [values],
        count,
        pl.BlockSpec((groups, 1, rows, width), lambda k, p: (0, index_of(k, p[0], count), 0, 0)),
        pl.BlockSpec((1, groups, rows, width), lambda k, p: (k, 0, 0, 0)),
        (count, groups, rows, width),
        LOW,
    )


def feed_forward(a_ref, dy_ref, fc_ref, proj_ref, bias_ref, out_ref, da_ref, dfc_ref, dproj_ref, db_ref):
    a_second, dy, fc, proj = a_ref[...], dy_ref[...], fc_ref[...], proj_ref[...]
    upper = dot(a_second, fc, NT) + bias_ref[...]
    square = upper * upper
    curve = jnp.tanh(0.7978845608028654 * (upper + 0.044715 * upper * square))
    rise = 0.5 * (1.0 + curve)
    active = (upper * rise).astype(LOW)
    slope = rise + 0.5 * upper * (1.0 - curve * curve) * (
        0.7978845608028654 * (1.0 + 3.0 * 0.044715 * square)
    )
    d_upper = dot(dy, proj, NT) * slope
    db_ref[...] = jnp.sum(d_upper, axis=0, keepdims=True)
    d_upper = d_upper.astype(LOW)
    out, d_a = dot(active, proj), dot(d_upper, fc)

    @pl.when(pl.program_id(0) == 0)
    def _():
        out_ref[...] = out
        da_ref[...] = d_a

    @pl.when(pl.program_id(0) > 0)
    def _():
        out_ref[...] += out
        da_ref[...] += d_a

    dproj_ref[...] = dot(active, dy, TN).astype(LOW)
    dfc_ref[...] = dot(d_upper, a_second, TN).astype(LOW)


def feed_forward_call(a_second, dy, fc, proj, bias):
    tokens, width = a_second.shape
    hidden = fc.shape[0]
    whole = pl.BlockSpec((tokens, width), lambda g: (0, 0))
    some = pl.BlockSpec((BLOCK, width), lambda g: (g, 0))
    row = pl.BlockSpec((1, BLOCK), lambda g: (0, g))
    return pl.pallas_call(
        feed_forward,
        grid=(hidden // BLOCK,),
        in_specs=[whole, whole, some, some, row],
        out_specs=[whole, whole, some, some, row],
        out_shape=[
            jax.ShapeDtypeStruct((tokens, width), WIDE),
            jax.ShapeDtypeStruct((tokens, width), WIDE),
            jax.ShapeDtypeStruct((hidden, width), LOW),
            jax.ShapeDtypeStruct((hidden, width), LOW),
            jax.ShapeDtypeStruct((1, hidden), WIDE),
        ],
        compiler_params=pltpu.CompilerParams(vmem_limit_bytes=VMEM),
        cost_estimate=pl.CostEstimate(
            flops=12 * tokens * hidden * width,
            bytes_accessed=8 * hidden * width + 12 * tokens * width,
            transcendentals=tokens * hidden,
        ),
        name="feed_forward",
    )(a_second, dy, fc, proj, bias)


def shards(
    inputs,
    gain1,
    bias1,
    w_qkv,
    bias_q,
    bias_v,
    w_out,
    bias_out,
    gain2,
    bias2,
    w_fc,
    bias_fc,
    w_proj,
    bias_proj,
    cotangent,
):
    n_dp, n_t = lax.axis_size("dp"), lax.axis_size("tensor")
    place, me = lax.axis_index("dp"), lax.axis_index("tensor")
    count, width = inputs.shape
    local = w_qkv.shape[2]
    hidden = w_fc.shape[1]
    heads = local // HEAD
    scale = HEAD ** (-0.5)
    own = count // n_t
    half = lax.rem(me, 2)
    rows_q, rows_o, rows_f = width // n_dp, local // n_dp, hidden // n_dp
    true = index_of(jnp.arange(n_dp, dtype=jnp.int32), place, n_dp)
    where = slot_of(jnp.arange(n_dp, dtype=jnp.int32), place, n_dp)

    qkv_own = w_qkv.reshape(width, 3 * local)
    piece = lax.dynamic_slice_in_dim(qkv_own, place * rows_q, rows_q, 0)
    q_first = across(piece, 2, n_t)
    vector = across(jnp.concatenate([bias_q, bias_v, bias_fc]), 2, n_t)
    biases = [bias_fc, vector[2 * local :], across(bias_fc, 1, n_t), across(bias_fc, 3, n_t)]
    piece = lax.dynamic_slice_in_dim(w_out, place * rows_o, rows_o, 0)
    o_first = gather_tensor(piece, n_t)
    piece = lax.dynamic_slice_in_dim(w_fc, place * rows_f, rows_f, 1).T
    f_first = gather_tensor(piece, n_t)
    piece = lax.dynamic_slice_in_dim(w_proj, place * rows_f, rows_f, 0)
    j_first = gather_tensor(piece, n_t)
    qkv_other = by_index(gather_plane(q_first, n_dp), place, LOW).reshape(width, 3 * local)
    w_out_all = groups_by_index(gather_plane(o_first, n_dp), place).reshape(n_t * local, width)
    last = exchanges(n_dp)[-1]
    some = n_t * hidden // 2
    fc_mine = gather_near(f_first, n_dp)
    fc_theirs = swap(fc_mine, last).reshape(some, width)
    fc_mine = fc_mine.reshape(some, width)
    proj_mine = gather_near(j_first, n_dp)
    proj_theirs = swap(proj_mine, last).reshape(some, width)
    proj_mine = proj_mine.reshape(some, width)
    bias_fc_all = jnp.stack(biases).reshape(n_t, n_dp, rows_f)
    bias_fc_all = bias_fc_all.at[:, true].get(mode="promise_in_bounds")
    bias_fc_all = bias_fc_all.transpose(1, 0, 2).reshape(2, 1, some)

    x_seq = lax.dynamic_slice_in_dim(inputs, (me // 2) * LEN, LEN, 0).astype(WIDE)
    normed, _ = norm_parts(x_seq)
    a_first = (normed * gain1 + bias1).astype(LOW)

    def project(weight, add_q, add_v):
        proj = dot(weight, a_first, TT)
        query = (proj[:local] + add_q[:, None]) * scale
        values = proj[2 * local :] + add_v[:, None]
        proj = jnp.concatenate([query, proj[local : 2 * local], values], axis=0)
        return proj.astype(LOW).reshape(3, heads, HEAD, LEN)

    def halves(value):
        mine = lax.dynamic_slice_in_dim(value, half * own, own, value.ndim - 1)
        theirs = lax.dynamic_slice_in_dim(value, (1 - half) * own, own, value.ndim - 1)
        return mine, theirs

    proj_a = project(qkv_own, bias_q, bias_v)
    out_a, lse_a = attention(proj_a)
    mine_a, theirs_a = halves(out_a.reshape(local, LEN))
    theirs_a = across(theirs_a, 1, n_t)
    proj_b = project(qkv_other, vector[:local], vector[local : 2 * local])
    out_b, lse_b = attention(proj_b)
    mine_b, theirs_b = halves(out_b.reshape(local, LEN))
    theirs_b = across(theirs_b, 1, n_t)
    attn_low = jnp.concatenate([mine_a, mine_b, theirs_a, theirs_b], axis=0)

    x_own = lax.dynamic_slice_in_dim(inputs, me * own, own, 0).astype(WIDE)
    dy = lax.dynamic_slice_in_dim(cotangent, me * own, own, 0)
    resid = x_own + dot(attn_low, w_out_all, TN) + bias_out
    normed2, rstd2 = norm_parts(resid)
    a_second = (normed2 * gain2 + bias2).astype(LOW)
    mixed_a, d_second_a, dfc_mine, dproj_mine, sums_mine = feed_forward_call(
        a_second, dy, fc_mine, proj_mine, bias_fc_all[0]
    )
    mixed_b, d_second_b, dfc_theirs, dproj_theirs, sums_theirs = feed_forward_call(
        a_second, dy, fc_theirs, proj_theirs, bias_fc_all[1]
    )
    output = (resid + (mixed_a + mixed_b) + bias_proj).astype(LOW)
    d_resid_norm, d_gain2, d_bias2 = norm_back(normed2, rstd2, gain2, d_second_a + d_second_b)
    d_resid = dy.astype(WIDE) + d_resid_norm
    d_resid_low = d_resid.astype(LOW)
    d_attn = dot(w_out_all, d_resid_low, NT).astype(LOW)
    d_mine, d_theirs = d_attn[: 2 * local], d_attn[2 * local :]
    d_theirs = across(d_theirs, 1, n_t)
    d_out = jnp.where(
        half == 0,
        jnp.concatenate([d_mine, d_theirs], axis=1),
        jnp.concatenate([d_theirs, d_mine], axis=1),
    ).reshape(2, heads, HEAD, LEN)

    def reduce_hidden(mine, theirs):
        shape = (n_dp // 2, n_t, rows_f, width)
        total = sum_tensor(sum_plane(mine.reshape(shape), theirs.reshape(shape), n_dp), n_t)
        return by_index(gather_plane(total, n_dp), place, WIDE).reshape(hidden, width)

    d_w_proj = reduce_hidden(dproj_mine, dproj_theirs)
    d_w_fc = reduce_hidden(dfc_mine, dfc_theirs).T
    grad = dot(attn_low, d_resid_low).astype(LOW).reshape(n_t, n_dp, rows_o, width)
    grad = groups_by_slot(grad, place)
    total = sum_tensor(sum_plane(grad[: n_dp // 2], grad[n_dp // 2 :], n_dp), n_t)
    d_w_out = by_index(gather_plane(total, n_dp), place, WIDE).reshape(local, width)

    d_proj_a = attention_back(proj_a, out_a, d_out[0], lse_a).reshape(3 * local, LEN)
    d_proj_b = attention_back(proj_b, out_b, d_out[1], lse_b).reshape(3 * local, LEN)

    def d_first_of(begin):
        rows_a = lax.dynamic_slice_in_dim(d_proj_a, begin, own, 1)
        rows_b = lax.dynamic_slice_in_dim(d_proj_b, begin, own, 1)
        return dot(rows_a, qkv_own, TT) + dot(rows_b, qkv_other, TT)

    d_theirs = across(d_first_of((1 - half) * own).astype(LOW), 1, n_t)
    d_first = d_first_of(half * own) + d_theirs.astype(WIDE)
    normed1, rstd1 = norm_parts(x_own)
    d_in_norm, d_gain1, d_bias1 = norm_back(normed1, rstd1, gain1, d_first)
    d_inputs = (d_resid + d_in_norm).astype(LOW)

    def by_rows(d_proj):
        return dot(a_first, d_proj, TT).astype(LOW).reshape(n_dp, rows_q, 3 * local)

    grad = by_slot_two(by_rows(d_proj_a), by_rows(d_proj_b), place)
    total = sum_plane(grad[: n_dp // 2], grad[n_dp // 2 :], n_dp)
    total = add_low(total[0], across(total[1], 2, n_t))
    d_w_qkv = by_index(gather_plane(total, n_dp), place, WIDE).reshape(width, 3, local)

    sums_a = jnp.sum(d_proj_a.reshape(3, local, LEN).astype(WIDE), axis=2)
    sums_b = jnp.sum(d_proj_b.reshape(3, local, LEN).astype(WIDE), axis=2)
    group = jnp.arange(n_t, dtype=jnp.int32)[None, :, None]
    bias_rows = jnp.where(group == me, sums_a[:, None], 0.0)
    bias_rows += jnp.where(group == (me ^ 2), sums_b[:, None], 0.0)
    sums_fc = jnp.stack([sums_mine, sums_theirs]).reshape(n_dp, n_t, rows_f)
    sums_fc = sums_fc.at[where].get(mode="promise_in_bounds")
    sums_fc = sum(
        jnp.where(group[0, :, None] == (me ^ mask), sums_fc[None, :, at], 0.0)
        for at, mask in enumerate(ORDER)
    )
    vectors = jnp.concatenate(
        [
            d_gain1,
            d_bias1,
            d_gain2,
            d_bias2,
            jnp.sum(d_resid, axis=0),
            jnp.sum(dy.astype(WIDE), axis=0),
            bias_rows[0].reshape(-1),
            bias_rows[2].reshape(-1),
            sums_fc.reshape(-1),
        ]
    ).reshape(-1, 128)
    for mask in (1, 2):
        vectors = vectors + across(vectors, mask, n_t)
    for step in exchanges(n_dp):
        vectors = vectors + swap(vectors, step)
    vectors = vectors.reshape(-1, width)
    d_gain1, d_bias1, d_gain2, d_bias2, d_bias_out, d_bias_proj = (vectors[r] for r in range(6))
    d_bias_q = lax.dynamic_slice_in_dim(vectors[6], me * local, local, 0)
    d_bias_v = lax.dynamic_slice_in_dim(vectors[7], me * local, local, 0)
    d_bias_fc = lax.dynamic_slice_in_dim(vectors[8:].reshape(-1), me * hidden, hidden, 0)
    return (
        ring_tensor(output, n_t),
        ring_tensor(d_inputs, n_t),
        d_gain1,
        d_bias1,
        d_w_qkv,
        d_bias_q,
        d_bias_v,
        d_w_out,
        d_bias_out,
        d_gain2,
        d_bias2,
        d_w_fc,
        d_bias_fc,
        d_w_proj,
        d_bias_proj,
    )


def solution(mesh):
    placed = (
        P("dp", None),
        P(),
        P(),
        P(None, None, "tensor"),
        P("tensor"),
        P("tensor"),
        P("tensor", None),
        P(),
        P(),
        P(),
        P(None, "tensor"),
        P("tensor"),
        P("tensor", None),
        P(),
        P("dp", None),
    )
    return jax.shard_map(
        shards,
        mesh=mesh,
        in_specs=placed,
        out_specs=(
            P("dp", None),
            P("dp", None),
            P(),
            P(),
            P(None, None, "tensor"),
            P("tensor"),
            P("tensor"),
            P("tensor", None),
            P(),
            P(),
            P(),
            P(None, "tensor"),
            P("tensor"),
            P("tensor", None),
            P(),
        ),
        check_vma=False,
    )
```

```python
import jax
import jax.numpy as jnp
from jax import lax
from jax.experimental import pallas as pl
from jax.experimental.pallas import tpu as pltpu
from jax.sharding import PartitionSpec as P

HEAD = 64
LEN = 1024
BLOCK = 256
UNITS = 768
VMEM = 32 * 2**20
SMALL = pl.CostEstimate(flops=1, bytes_accessed=1, transcendentals=0)


LOW = jnp.bfloat16
WIDE = jnp.float32

NN = (((1,), (0,)), ((), ()))
NT = (((1,), (1,)), ((), ()))
TN = (((0,), (0,)), ((), ()))
TT = (((0,), (1,)), ((), ()))


def dot(left, right, dims=NN):
    return lax.dot_general(left, right, dims, preferred_element_type=WIDE)


def norm_parts(value):
    centre = value - jnp.mean(value, axis=-1, keepdims=True)
    rstd = lax.rsqrt(jnp.mean(centre * centre, axis=-1, keepdims=True) + 1e-05)
    return (centre * rstd, rstd)


def norm_back(normed, rstd, gain, grad):
    scaled = grad * gain
    inner = (
        scaled
        - jnp.mean(scaled, axis=-1, keepdims=True)
        - normed * jnp.mean(scaled * normed, axis=-1, keepdims=True)
    )
    return (rstd * inner, jnp.sum(grad * normed, axis=0), jnp.sum(grad, axis=0))


def causal(scores):
    keys = lax.broadcasted_iota(jnp.int32, scores.shape, 0)
    queries = lax.broadcasted_iota(jnp.int32, scores.shape, 1)
    return keys <= queries


def attend(q_ref, k_ref, v_ref, o_ref, lse_ref):
    query, values = q_ref[0, 0], v_ref[0, 0]
    keys = k_ref[0, 0].T
    for lo in range(0, LEN, BLOCK):
        hi = lo + BLOCK
        near = dot(keys[lo:hi], query[:, lo:hi])
        near = jnp.where(causal(near), near, -1e30)
        top = jnp.max(near, axis=0, keepdims=True)
        if lo:
            far = dot(keys[:lo], query[:, lo:hi])
            top = jnp.maximum(top, jnp.max(far, axis=0, keepdims=True))
        near = jnp.exp(near - top)
        total = jnp.sum(near, axis=0, keepdims=True)
        out = dot(values[:, lo:hi], near.astype(LOW))
        if lo:
            far = jnp.exp(far - top)
            total += jnp.sum(far, axis=0, keepdims=True)
            out += dot(values[:, :lo], far.astype(LOW))
        o_ref[0, :, lo:hi] = (out / total).astype(LOW)
        lse_ref[0, :, lo:hi] = top + jnp.log(total)


def attend_back(q_ref, k_ref, v_ref, o_ref, do_ref, lse_ref, *refs):
    out_ref, dq_ref = refs[-2:]
    query, keys_t, d_out = q_ref[0, 0], k_ref[0, 0], do_ref[0]
    keys, values = keys_t.T, v_ref[0, 0].T
    lse = lse_ref[0]
    delta = jnp.sum(d_out.astype(WIDE) * o_ref[0].astype(WIDE), axis=0, keepdims=True)

    def part(lo, hi, begin, end, mask):
        probs = jnp.exp(dot(keys[lo:hi], query[:, begin:end]) - lse[:, begin:end])
        if mask:
            probs = jnp.where(causal(probs), probs, 0.0)
        d_probs = dot(values[lo:hi], d_out[:, begin:end])
        d_scores = (probs * (d_probs - delta[:, begin:end])).astype(LOW)
        d_values = dot(d_out[:, begin:end], probs.astype(LOW), NT)
        d_keys = dot(query[:, begin:end], d_scores, NT)
        d_query = dot(keys_t[:, lo:hi], d_scores)
        if lo == 0:
            dq_ref[:, begin:end] = d_query
        else:
            dq_ref[:, begin:end] += d_query
        return d_keys, d_values

    for lo in range(0, LEN, BLOCK):
        hi = lo + BLOCK
        d_keys, d_values = part(lo, hi, lo, hi, True)
        if hi < LEN:
            more_keys, more_values = part(lo, hi, hi, LEN, False)
            d_keys += more_keys
            d_values += more_values
        out_ref[1, 0, :, lo:hi] = d_keys.astype(LOW)
        out_ref[2, 0, :, lo:hi] = d_values.astype(LOW)
    d_query = dq_ref[...].astype(LOW).astype(WIDE) * HEAD ** (-0.5)
    out_ref[0, 0] = d_query.astype(LOW)


ANY = pl.BlockSpec(memory_space=pl.ANY)


def kind(which):
    return pl.BlockSpec((1, 1, HEAD, LEN), lambda head: (which, head, 0, 0))


QKV = [kind(0), kind(1), kind(2)]
PER_HEAD = pl.BlockSpec((1, HEAD, LEN), lambda head: (head, 0, 0))
PER_ROW = pl.BlockSpec((1, 1, LEN), lambda head: (head, 0, 0))


def attention(qkv):
    heads = qkv.shape[1]
    return pl.pallas_call(
        attend,
        grid=(heads,),
        in_specs=QKV,
        out_specs=[PER_HEAD, PER_ROW],
        out_shape=[
            jax.ShapeDtypeStruct((heads, HEAD, LEN), LOW),
            jax.ShapeDtypeStruct((heads, 1, LEN), WIDE),
        ],
        compiler_params=pltpu.CompilerParams(vmem_limit_bytes=VMEM),
        cost_estimate=SMALL,
        name="attention",
    )(qkv, qkv, qkv)


def attention_back(qkv, out, d_out, lse, *earlier):
    heads = qkv.shape[1]
    return pl.pallas_call(
        attend_back,
        grid=(heads,),
        in_specs=QKV + [PER_HEAD, PER_HEAD, PER_ROW] + [ANY] * len(earlier),
        out_specs=pl.BlockSpec((3, 1, HEAD, LEN), lambda head: (0, head, 0, 0)),
        out_shape=jax.ShapeDtypeStruct((3, heads, HEAD, LEN), LOW),
        scratch_shapes=[pltpu.VMEM((HEAD, LEN), WIDE)],
        compiler_params=pltpu.CompilerParams(vmem_limit_bytes=VMEM),
        cost_estimate=SMALL,
        name="attention_back",
    )(qkv, qkv, qkv, out, d_out, lse, *earlier)


def bits(size, odd):
    above = [1 << b for b in range(1, size.bit_length() - 1)]
    return above if odd else above[::-1]


def exchanges(size):
    steps = [
        [(d, d ^ (odd if d & 1 else even)) for d in range(size)]
        for even, odd in zip(bits(size, False), bits(size, True))
    ]
    return steps + [[(d, d ^ 1) for d in range(size)]]


def turned(value, size, odd):
    count = size.bit_length() - 2
    back = value * 0
    for b in range(count):
        back = back | (((value >> b) & 1) << (count - 1 - b))
    return jnp.where(odd == 1, value, back)


def slot_of(index, place, size):
    mask = index ^ place
    low = mask & 1
    return low * (size // 2) + turned(mask >> 1, size, (place & 1) ^ low)


def index_of(slot, place, size):
    low = slot // (size // 2)
    return ((turned(slot % (size // 2), size, (place & 1) ^ low) << 1) | low) ^ place


def swap(value, step):
    return lax.ppermute(value, "dp", step)


def add_low(left, right):
    return (left.astype(WIDE) + right.astype(WIDE)).astype(LOW)


def across(piece, mask, size):
    return lax.ppermute(piece, "tensor", [(t, t ^ mask) for t in range(size)])


ORDER = (0, 2, 1, 3)


def to_others(piece, size):
    return [across(piece, m, size) for m in ORDER[1:]]


def nothing(*refs):
    pass


def after(value, *earlier):
    return pl.pallas_call(
        nothing,
        in_specs=[ANY] * (1 + len(earlier)),
        out_specs=ANY,
        out_shape=jax.ShapeDtypeStruct(value.shape, value.dtype),
        input_output_aliases={0: 0},
        cost_estimate=SMALL,
        name="after",
    )(value, *earlier)


def to_right(piece, size):
    return lax.ppermute(piece, "tensor", [(t, (t + 1) % size) for t in range(size)])


def to_left(piece, size):
    return lax.ppermute(piece, "tensor", [(t, (t - 1) % size) for t in range(size)])


def onward(pair, size):
    rows = pair[0].shape[0] // 2
    return to_right(pair[0][:rows], size), to_left(pair[1][rows:], size)


def assemble(me_ref, own_ref, left_ref, right_ref, first_ref, second_ref, out_ref):
    step, rows = pl.program_id(0), first_ref.shape[0]

    @pl.when(step == 0)
    def _():
        out_ref[...] = own_ref[...]

    @pl.when(step == 1)
    def _():
        out_ref[...] = left_ref[...]

    @pl.when(step == 2)
    def _():
        out_ref[:rows] = first_ref[...]
        out_ref[rows:] = second_ref[...]

    @pl.when(step == 3)
    def _():
        out_ref[...] = right_ref[...]


def assembled(own, near, far):
    size = 4
    rows, width = own.shape
    full = pl.BlockSpec((rows, width), lambda g, me: (0, 0))
    part = pl.BlockSpec((rows // 2, width), lambda g, me: (0, 0))
    return pl.pallas_call(
        assemble,
        grid_spec=pltpu.PrefetchScalarGridSpec(
            num_scalar_prefetch=1,
            grid=(size,),
            in_specs=[full, full, full, part, part],
            out_specs=pl.BlockSpec(
                (rows, width), lambda g, me: (lax.rem(me[0] - g + size, size), 0)
            ),
        ),
        out_shape=jax.ShapeDtypeStruct((size * rows, width), own.dtype),
        compiler_params=pltpu.CompilerParams(vmem_limit_bytes=VMEM),
        name="assemble",
    )(lax.axis_index("tensor")[None], own, *near, *far)


def pick(place_ref, *refs):
    for at, in_ref in enumerate(refs[:-1]):
        value = in_ref[...]
        refs[-1][...] = value.reshape(refs[-1].shape).astype(refs[-1].dtype)


def reorder_call(kernel, place, values, earlier, count, in_spec, out_spec, shape, dtype):
    return pl.pallas_call(
        kernel,
        grid_spec=pltpu.PrefetchScalarGridSpec(
            num_scalar_prefetch=1,
            grid=(count,),
            in_specs=[in_spec] * len(values) + [ANY] * len(earlier),
            out_specs=out_spec,
        ),
        out_shape=jax.ShapeDtypeStruct(shape, dtype),
        compiler_params=pltpu.CompilerParams(vmem_limit_bytes=VMEM),
        name="reorder",
    )(place[None], *values, *earlier)


def by_index(slots, place, dtype):
    count, rows, width = slots.shape
    return reorder_call(
        pick,
        place,
        [slots],
        (),
        count,
        pl.BlockSpec((1, rows, width), lambda j, p: (slot_of(j, p[0], count), 0, 0)),
        pl.BlockSpec((1, rows, width), lambda j, p: (j, 0, 0)),
        slots.shape,
        dtype,
    )


def split_two(place_ref, in_ref, first_ref, second_ref):
    first_ref[0] = in_ref[0, 0].astype(first_ref.dtype)
    second_ref[0] = in_ref[1, 0].astype(second_ref.dtype)


def two_by_index(slots, place):
    _, count, rows, width = slots.shape
    one = pl.BlockSpec((1, rows, width), lambda j, p: (j, 0, 0))
    shape = jax.ShapeDtypeStruct((count, rows, width), WIDE)
    return pl.pallas_call(
        split_two,
        grid_spec=pltpu.PrefetchScalarGridSpec(
            num_scalar_prefetch=1,
            grid=(count,),
            in_specs=[
                pl.BlockSpec((2, 1, rows, width), lambda j, p: (0, slot_of(j, p[0], count), 0, 0))
            ],
            out_specs=[one, one],
        ),
        out_shape=[shape, shape],
        compiler_params=pltpu.CompilerParams(vmem_limit_bytes=VMEM),
        name="reorder",
    )(place[None], slots)


def groups_by_index(slots, place):
    count, groups, rows, width = slots.shape
    return reorder_call(
        pick,
        place,
        [slots],
        (),
        count,
        pl.BlockSpec((1, groups, rows, width), lambda j, p: (slot_of(j, p[0], count), 0, 0, 0)),
        pl.BlockSpec((groups, 1, rows, width), lambda j, p: (0, j, 0, 0)),
        (groups, count, rows, width),
        LOW,
    )


def groups_by_slot(values, place):
    groups, count, rows, width = values.shape
    return reorder_call(
        pick,
        place,
        [values],
        (),
        count,
        pl.BlockSpec((groups, 1, rows, width), lambda k, p: (0, index_of(k, p[0], count), 0, 0)),
        pl.BlockSpec((1, groups, rows, width), lambda k, p: (k, 0, 0, 0)),
        (count, groups, rows, width),
        LOW,
    )


def middle(
    attn_ref, w_out_ref, x_ref, dy_ref, rows_ref, w_ref, bias_ref,
    out_ref, mine_ref, theirs_ref, resid_ref, dw_out_ref, sums_ref, dw_ref, db_ref,
    a_ref, normed_ref, rstd_ref, mixed_ref, da_ref,
):
    @pl.when(pl.program_id(0) == 0)
    def _():
        resid = x_ref[...].astype(WIDE) + dot(attn_ref[...], w_out_ref[...], TN) + rows_ref[0:1]
        normed, rstd = norm_parts(resid)
        resid_ref[...] = resid
        normed_ref[...] = normed
        rstd_ref[...] = rstd
        a_ref[...] = (normed * rows_ref[1:2] + rows_ref[2:3]).astype(LOW)
        mixed_ref[...] = jnp.zeros_like(mixed_ref)
        da_ref[...] = jnp.zeros_like(da_ref)

    a_second, dy = a_ref[...], dy_ref[...]
    for lo in range(0, UNITS, BLOCK):
        some = slice(lo, lo + BLOCK)
        fc, proj = w_ref[0, some], w_ref[1, some]
        upper = dot(a_second, fc, NT) + bias_ref[:, some]
        square = upper * upper
        curve = jnp.tanh(0.7978845608028654 * (upper + 0.044715 * upper * square))
        rise = 0.5 * (1.0 + curve)
        active = (upper * rise).astype(LOW)
        slope = rise + 0.5 * upper * (1.0 - curve * curve) * (
            0.7978845608028654 * (1.0 + 3.0 * 0.044715 * square)
        )
        d_upper = dot(dy, proj, NT) * slope
        db_ref[:, some] = jnp.sum(d_upper, axis=0, keepdims=True)
        d_upper = d_upper.astype(LOW)
        mixed_ref[...] += dot(active, proj)
        da_ref[...] += dot(d_upper, fc)
        grads = (dot(d_upper, a_second, TN).astype(LOW), dot(active, dy, TN).astype(LOW))
        rows = dw_ref.shape[2]
        for slot in range(lo // rows, -(-(lo + BLOCK) // rows)):
            first, end = max(lo, slot * rows), min(lo + BLOCK, (slot + 1) * rows)
            place = slice(first - slot * rows, end - slot * rows)
            for which, grad in enumerate(grads):
                dw_ref[slot, which, place] = grad[first - lo : end - lo]

    @pl.when(pl.program_id(0) == pl.num_programs(0) - 1)
    def _():
        out_ref[...] = (resid_ref[...] + mixed_ref[...] + rows_ref[3:4]).astype(LOW)
        d_resid, d_gain, d_bias = norm_back(
            normed_ref[...], rstd_ref[...], rows_ref[1:2], da_ref[...]
        )
        dy_wide = dy_ref[...].astype(WIDE)
        d_resid += dy_wide
        resid_ref[...] = d_resid
        sums_ref[0:1] = d_gain[None]
        sums_ref[1:2] = d_bias[None]
        sums_ref[2:3] = jnp.sum(d_resid, axis=0, keepdims=True)
        sums_ref[3:4] = jnp.sum(dy_wide, axis=0, keepdims=True)
        sums_ref[4:8] = jnp.zeros_like(sums_ref[4:8])
        low = d_resid.astype(LOW)
        split = mine_ref.shape[0]
        mine_ref[...] = dot(w_out_ref[:split], low, NT).astype(LOW)
        theirs_ref[...] = dot(w_out_ref[split:], low, NT).astype(LOW)
        dw_out_ref[...] = dot(attn_ref[...], low).astype(LOW)


def middle_call(attn, w_out, x, dy, rows, weights, bias, parts):
    tokens, width = x.shape
    hidden = weights.shape[1]
    once = pl.Buffered(1)

    def whole(*shape):
        return pl.BlockSpec(shape, lambda g: (0,) * len(shape), pipeline_mode=once)

    some = pl.BlockSpec((2, UNITS, width), lambda g: (0, g, 0))
    each = hidden // parts
    slots = pl.BlockSpec((UNITS // each, 2, each, width), lambda g: (g, 0, 0, 0))
    row = pl.BlockSpec((1, UNITS), lambda g: (0, g))
    local = attn.shape[0] // 2
    return pl.pallas_call(
        middle,
        grid=(hidden // UNITS,),
        in_specs=[
            whole(*attn.shape),
            whole(*w_out.shape),
            whole(tokens, width),
            whole(tokens, width),
            whole(*rows.shape),
            some,
            row,
        ],
        out_specs=[
            whole(tokens, width),
            whole(local, tokens),
            whole(local, tokens),
            whole(tokens, width),
            whole(*w_out.shape),
            whole(8, width),
            slots,
            row,
        ],
        out_shape=[
            jax.ShapeDtypeStruct((tokens, width), LOW),
            jax.ShapeDtypeStruct((local, tokens), LOW),
            jax.ShapeDtypeStruct((local, tokens), LOW),
            jax.ShapeDtypeStruct((tokens, width), WIDE),
            jax.ShapeDtypeStruct(w_out.shape, LOW),
            jax.ShapeDtypeStruct((8, width), WIDE),
            jax.ShapeDtypeStruct((parts, 2, each, width), LOW),
            jax.ShapeDtypeStruct((1, hidden), WIDE),
        ],
        scratch_shapes=[
            pltpu.VMEM((tokens, width), LOW),
            pltpu.VMEM((tokens, width), WIDE),
            pltpu.VMEM((tokens, 1), WIDE),
            pltpu.VMEM((tokens, width), WIDE),
            pltpu.VMEM((tokens, width), WIDE),
        ],
        compiler_params=pltpu.CompilerParams(vmem_limit_bytes=48 * 2**20),
        cost_estimate=SMALL,
        name="middle",
    )(attn, w_out, x, dy, rows, weights, bias)


def first_back(half_ref, d_a_ref, d_b_ref, w_a_ref, w_b_ref, *refs):
    mine_ref, theirs_ref = refs[-2:]
    own = mine_ref.shape[0]
    for out_ref, which in ((theirs_ref, 1 - half_ref[0]), (mine_ref, half_ref[0])):
        some = pl.ds(pl.multiple_of(which * own, own), own)
        value = dot(d_a_ref[:, some], w_a_ref[...], TN) + dot(d_b_ref[:, some], w_b_ref[...], TN)
        out_ref[...] = value.astype(out_ref.dtype)


def first_back_call(half, d_a, d_b, w_a, w_b, own, *earlier):
    width = w_a.shape[1]

    def whole(*shape):
        return pl.BlockSpec(shape, lambda g, h: (0,) * len(shape))

    return pl.pallas_call(
        first_back,
        grid_spec=pltpu.PrefetchScalarGridSpec(
            num_scalar_prefetch=1,
            grid=(1,),
            in_specs=[whole(*v.shape) for v in (d_a, d_b, w_a, w_b)] + [ANY] * len(earlier),
            out_specs=[whole(own, width), whole(own, width)],
        ),
        out_shape=[
            jax.ShapeDtypeStruct((own, width), WIDE),
            jax.ShapeDtypeStruct((own, width), LOW),
        ],
        compiler_params=pltpu.CompilerParams(vmem_limit_bytes=VMEM),
        cost_estimate=SMALL,
        name="first_back",
    )(half[None], d_a, d_b, w_a, w_b, *earlier)


def weight_back(place_ref, a_ref, d_a_ref, d_b_ref, *refs):
    refs[-1][0, 0] = dot(a_ref[0], d_a_ref[...], NT).astype(LOW)
    refs[-1][0, 1] = dot(a_ref[0], d_b_ref[...], NT).astype(LOW)


def weight_back_call(place, a_first, d_a, d_b, *earlier):
    count, rows, tokens = a_first.shape
    columns = d_a.shape[0]
    whole = pl.BlockSpec((columns, tokens), lambda k, p: (0, 0))
    return pl.pallas_call(
        weight_back,
        grid_spec=pltpu.PrefetchScalarGridSpec(
            num_scalar_prefetch=1,
            grid=(count,),
            in_specs=[
                pl.BlockSpec((1, rows, tokens), lambda k, p: (index_of(k, p[0], count), 0, 0)),
                whole,
                whole,
            ]
            + [ANY] * len(earlier),
            out_specs=pl.BlockSpec((1, 2, rows, columns), lambda k, p: (k, 0, 0, 0)),
        ),
        out_shape=jax.ShapeDtypeStruct((count, 2, rows, columns), LOW),
        compiler_params=pltpu.CompilerParams(vmem_limit_bytes=VMEM),
        cost_estimate=SMALL,
        name="weight_back",
    )(place[None], a_first, d_a, d_b, *earlier)


def shards(
    inputs,
    gain1,
    bias1,
    w_qkv,
    bias_q,
    bias_v,
    w_out,
    bias_out,
    gain2,
    bias2,
    w_fc,
    bias_fc,
    w_proj,
    bias_proj,
    cotangent,
):
    n_dp, n_t = lax.axis_size("dp"), lax.axis_size("tensor")
    place, me = lax.axis_index("dp"), lax.axis_index("tensor")
    count, width = inputs.shape
    local = w_qkv.shape[2]
    hidden = w_fc.shape[1]
    heads = local // HEAD
    scale = HEAD ** (-0.5)
    own = count // n_t
    half = lax.rem(me, 2)
    rows_q, rows_o, rows_f = width // n_dp, local // n_dp, hidden // n_dp

    plane = exchanges(n_dp)
    near, last = plane[:-1], plane[-1]

    qkv_own = w_qkv.reshape(width, 3 * local)
    q = across(lax.dynamic_slice_in_dim(qkv_own, place * rows_q, rows_q, 0), 2, n_t)
    vector = across(jnp.concatenate([bias_q, bias_v, bias_fc]), 2, n_t)
    biases = [bias_fc, vector[2 * local :], across(bias_fc, 1, n_t), across(bias_fc, 3, n_t)]
    o = lax.dynamic_slice_in_dim(w_out, place * rows_o, rows_o, 0)
    o_parts = to_others(o, n_t)
    w = jnp.stack(
        [
            lax.dynamic_slice_in_dim(w_fc, place * rows_f, rows_f, 1).T,
            lax.dynamic_slice_in_dim(w_proj, place * rows_f, rows_f, 0),
        ]
    )
    w = lax.all_gather(w, ("dp", "tensor"), axis=1, tiled=True)

    x_seq = lax.dynamic_slice_in_dim(inputs, (me // 2) * LEN, LEN, 0).astype(WIDE)
    normed, _ = norm_parts(x_seq)
    a_first = (normed * gain1 + bias1).astype(LOW)

    def project(weight, add_q, add_v):
        proj = dot(weight, a_first, TT)
        query = (proj[:local] + add_q[:, None]) * scale
        values = proj[2 * local :] + add_v[:, None]
        proj = jnp.concatenate([query, proj[local : 2 * local], values], axis=0)
        return proj.astype(LOW).reshape(3, heads, HEAD, LEN)

    def halves(value):
        mine = lax.dynamic_slice_in_dim(value, half * own, own, value.ndim - 1)
        theirs = lax.dynamic_slice_in_dim(value, (1 - half) * own, own, value.ndim - 1)
        return mine, theirs

    def both(held, step, axis=0):
        return jnp.concatenate([held, swap(held, step)], axis=axis)

    q, o = q[None], jnp.stack([o] + o_parts)[None]
    for step in near:
        q = both(q, step)
    q_take = swap(q, last)
    proj_a = project(qkv_own, bias_q, bias_v)
    out_a, lse_a = attention(proj_a)
    mine_a, theirs_a = halves(out_a.reshape(local, LEN))
    theirs_a = across(theirs_a, 1, n_t)
    for step in plane:
        o = both(o, step)
    qkv_other = by_index(jnp.concatenate([q, q_take], axis=0), place, LOW)
    qkv_other = qkv_other.reshape(width, 3 * local)
    proj_b = project(qkv_other, vector[:local], vector[local : 2 * local])
    out_b, lse_b = attention(proj_b)
    mine_b, theirs_b = halves(out_b.reshape(local, LEN))
    theirs_b = across(theirs_b, 1, n_t)
    w_out_all = groups_by_index(o, place).reshape(n_t * local, width)
    attn_low = jnp.concatenate([mine_a, mine_b, theirs_a, theirs_b], axis=0)
    place_of = jnp.array([ORDER.index(m) for m in range(n_t)], jnp.int32)
    place_of = place_of[jnp.arange(n_t, dtype=jnp.int32) ^ me]
    bias_fc_all = jnp.stack(biases).reshape(n_t, n_dp, rows_f)
    bias_fc_all = bias_fc_all.at[place_of].get(mode="promise_in_bounds")
    bias_fc_all = bias_fc_all.transpose(1, 0, 2).reshape(1, n_t * hidden)

    x_own = lax.dynamic_slice_in_dim(inputs, me * own, own, 0)
    dy = lax.dynamic_slice_in_dim(cotangent, me * own, own, 0)
    rows = jnp.stack([bias_out, gain2, bias2, bias_proj])
    output, d_mine, d_theirs, d_resid, o, sums_row, w, sums_fc = middle_call(
        attn_low, w_out_all, x_own, dy, rows, w, bias_fc_all, n_dp
    )
    from_left = to_right(output, n_t)
    d_take = across(d_theirs, 1, n_t)
    output_near = (from_left, to_left(after(output, d_take), n_t))

    def parted(held, axis=0):
        middle = held.shape[axis] // 2
        return jnp.split(held, [middle], axis=axis)

    def folded(held, taken, axis=0):
        held, taken = parted(held, axis), parted(taken, axis)
        return add_low(held[0], taken[0]), add_low(held[1], taken[1])

    w = lax.psum_scatter(w, "dp")
    o, o_send = parted(groups_by_slot(o.reshape(n_t, n_dp, rows_o, width), place))
    o_take = swap(o_send, last)
    d_out = jnp.where(
        half == 0,
        jnp.concatenate([d_mine, d_take], axis=1),
        jnp.concatenate([d_take, d_mine], axis=1),
    )
    d_out = d_out.reshape(2, heads, HEAD, LEN)

    down = near[::-1]
    d_proj_a = attention_back(proj_a, out_a, d_out[0], lse_a)
    d_proj_b = attention_back(proj_b, out_b, d_out[1], lse_b, d_proj_a)
    d_proj_a = d_proj_a.reshape(3 * local, LEN)
    d_proj_b = d_proj_b.reshape(3 * local, LEN)

    d_first, d_theirs = first_back_call(
        half, d_proj_a, d_proj_b, qkv_own.T, qkv_other.T, own, *output_near
    )
    d_first_take = across(d_theirs, 1, n_t)
    output_near = tuple(after(part, d_theirs) for part in output_near)
    output_far = onward(output_near, n_t)

    a_rows = a_first.T.reshape(n_dp, rows_q, LEN)
    q, q_send = parted(weight_back_call(place, a_rows, d_proj_a, d_proj_b, d_theirs))
    q_take = swap(q_send, last)
    o, o_send = folded(o, after(o_take, d_theirs))
    for step in down:
        o_take = swap(o_send, step)
        if step is not down[-1]:
            o, o_send = folded(o, o_take)
    sums_a = jnp.sum(d_proj_a.reshape(3, local, LEN).astype(WIDE), axis=2)
    sums_b = jnp.sum(d_proj_b.reshape(3, local, LEN).astype(WIDE), axis=2)
    group = jnp.arange(n_t, dtype=jnp.int32)[None, :, None]
    bias_rows = jnp.where(group == me, sums_a[:, None], 0.0)
    bias_rows += jnp.where(group == (me ^ 2), sums_b[:, None], 0.0)
    sums_fc = sums_fc.reshape(n_dp, n_t, rows_f).transpose(1, 0, 2)
    w = w.reshape(2, n_t, rows_f, width)
    w = [lax.dynamic_index_in_dim(w, me ^ m, 1, keepdims=False) for m in ORDER]
    w_parts = [across(w[at], m, n_t) for at, m in enumerate(ORDER) if at]
    normed1, rstd1 = norm_parts(x_own.astype(WIDE))
    d_first = d_first + d_first_take.astype(WIDE)
    d_in_norm, d_gain1, d_bias1 = norm_back(normed1, rstd1, after(gain1, *output_far, *w[1:]), d_first)
    d_inputs = (d_resid + d_in_norm).astype(LOW)
    inputs_near = to_right(d_inputs, n_t), to_left(d_inputs, n_t)

    def sum_tensor(held):
        return held[0], [across(held[at], m, n_t) for at, m in enumerate(ORDER) if at]

    def total_of(mine, parts):
        total = mine.astype(WIDE)
        for part in parts:
            total += part.astype(WIDE)
        return total.astype(LOW)

    o, o_parts = sum_tensor(add_low(o, o_take)[0])
    for step in down:
        q, q_send = folded(q, q_take)
        q_take = swap(q_send, step)
    q = add_low(q, q_take)[0]
    q_take = across(q[1], 2, n_t)
    vectors = jnp.concatenate(
        [
            d_gain1,
            d_bias1,
            sums_row[:4].reshape(-1),
            bias_rows[0].reshape(-1),
            bias_rows[2].reshape(-1),
            sums_fc.reshape(-1),
        ]
    ).reshape(-1, 128)
    inputs_far = onward(inputs_near, n_t)
    vectors = after(vectors, *inputs_near)
    for step in plane:
        vectors = vectors + swap(vectors, step)
    vectors = after(vectors, *inputs_far)
    for mask in (1, 2):
        vectors = vectors + across(vectors, mask, n_t)
    o = total_of(o, o_parts)[None]
    q = add_low(q[0], q_take)[None]
    for step in plane:
        o, q = both(o, step), both(q, step)
    w_parts[0] = after(w_parts[0], inputs_near[0])
    w = total_of(w[0], w_parts)[:, None]
    for step in plane:
        w = both(w, step, 1)
    d_w_out = by_index(o, place, WIDE).reshape(local, width)
    d_w_qkv = by_index(q, place, WIDE).reshape(width, 3, local)
    whole_output = assembled(output, output_near, output_far)
    whole_d_inputs = assembled(d_inputs, inputs_near, inputs_far)
    d_w_fc, d_w_proj = two_by_index(w, place)
    d_w_proj = d_w_proj.reshape(hidden, width)
    d_w_fc = d_w_fc.reshape(hidden, width).T
    vectors = vectors.reshape(-1, width)
    d_gain1, d_bias1, d_gain2, d_bias2, d_bias_out, d_bias_proj = (vectors[r] for r in range(6))
    d_bias_q = lax.dynamic_slice_in_dim(vectors[6], me * local, local, 0)
    d_bias_v = lax.dynamic_slice_in_dim(vectors[7], me * local, local, 0)
    d_bias_fc = lax.dynamic_slice_in_dim(vectors[8:].reshape(-1), me * hidden, hidden, 0)
    return (
        whole_output,
        whole_d_inputs,
        d_gain1,
        d_bias1,
        d_w_qkv,
        d_bias_q,
        d_bias_v,
        d_w_out,
        d_bias_out,
        d_gain2,
        d_bias2,
        d_w_fc,
        d_bias_fc,
        d_w_proj,
        d_bias_proj,
    )


def solution(mesh):
    placed = (
        P("dp", None),
        P(),
        P(),
        P(None, None, "tensor"),
        P("tensor"),
        P("tensor"),
        P("tensor", None),
        P(),
        P(),
        P(),
        P(None, "tensor"),
        P("tensor"),
        P("tensor", None),
        P(),
        P("dp", None),
    )
    return jax.shard_map(
        shards,
        mesh=mesh,
        in_specs=placed,
        out_specs=(
            P("dp", None),
            P("dp", None),
            P(),
            P(),
            P(None, None, "tensor"),
            P("tensor"),
            P("tensor"),
            P("tensor", None),
            P(),
            P(),
            P(),
            P(None, "tensor"),
            P("tensor"),
            P("tensor", None),
            P(),
        ),
        check_vma=False,
    )
```

```python
import jax
import jax.numpy as jnp
from jax import lax
from jax.experimental import pallas as pl
from jax.experimental.pallas import tpu as pltpu
from jax.sharding import PartitionSpec as P

HEAD = 64
LEN = 1024
BLOCK = 256
UNITS = 768
VMEM = 32 * 2**20
SMALL = pl.CostEstimate(flops=1, bytes_accessed=1, transcendentals=0)


LOW = jnp.bfloat16
WIDE = jnp.float32

NN = (((1,), (0,)), ((), ()))
NT = (((1,), (1,)), ((), ()))
TN = (((0,), (0,)), ((), ()))
TT = (((0,), (1,)), ((), ()))


def dot(left, right, dims=NN):
    return lax.dot_general(left, right, dims, preferred_element_type=WIDE)


def norm_parts(value):
    centre = value - jnp.mean(value, axis=-1, keepdims=True)
    rstd = lax.rsqrt(jnp.mean(centre * centre, axis=-1, keepdims=True) + 1e-05)
    return (centre * rstd, rstd)


def norm_back(normed, rstd, gain, grad):
    scaled = grad * gain
    inner = (
        scaled
        - jnp.mean(scaled, axis=-1, keepdims=True)
        - normed * jnp.mean(scaled * normed, axis=-1, keepdims=True)
    )
    return (rstd * inner, jnp.sum(grad * normed, axis=0), jnp.sum(grad, axis=0))


def causal(scores):
    keys = lax.broadcasted_iota(jnp.int32, scores.shape, 0)
    queries = lax.broadcasted_iota(jnp.int32, scores.shape, 1)
    return keys <= queries


def attend(q_ref, k_ref, v_ref, o_ref, lse_ref):
    query, values = q_ref[0, 0], v_ref[0, 0]
    keys = k_ref[0, 0].T
    for lo in range(0, LEN, BLOCK):
        hi = lo + BLOCK
        near = dot(keys[lo:hi], query[:, lo:hi])
        near = jnp.where(causal(near), near, -1e30)
        top = jnp.max(near, axis=0, keepdims=True)
        if lo:
            far = dot(keys[:lo], query[:, lo:hi])
            top = jnp.maximum(top, jnp.max(far, axis=0, keepdims=True))
        near = jnp.exp(near - top)
        total = jnp.sum(near, axis=0, keepdims=True)
        out = dot(values[:, lo:hi], near.astype(LOW))
        if lo:
            far = jnp.exp(far - top)
            total += jnp.sum(far, axis=0, keepdims=True)
            out += dot(values[:, :lo], far.astype(LOW))
        o_ref[0, :, lo:hi] = (out / total).astype(LOW)
        lse_ref[0, :, lo:hi] = top + jnp.log(total)


def attend_back(q_ref, k_ref, v_ref, o_ref, do_ref, lse_ref, *refs):
    out_ref, dq_ref = refs[-2:]
    query, keys_t, d_out = q_ref[0, 0], k_ref[0, 0], do_ref[0]
    keys, values = keys_t.T, v_ref[0, 0].T
    lse = lse_ref[0]
    delta = jnp.sum(d_out.astype(WIDE) * o_ref[0].astype(WIDE), axis=0, keepdims=True)

    def part(lo, hi, begin, end, mask):
        probs = jnp.exp(dot(keys[lo:hi], query[:, begin:end]) - lse[:, begin:end])
        if mask:
            probs = jnp.where(causal(probs), probs, 0.0)
        d_probs = dot(values[lo:hi], d_out[:, begin:end])
        d_scores = (probs * (d_probs - delta[:, begin:end])).astype(LOW)
        d_values = dot(d_out[:, begin:end], probs.astype(LOW), NT)
        d_keys = dot(query[:, begin:end], d_scores, NT)
        d_query = dot(keys_t[:, lo:hi], d_scores)
        if lo == 0:
            dq_ref[:, begin:end] = d_query
        else:
            dq_ref[:, begin:end] += d_query
        return d_keys, d_values

    for lo in range(0, LEN, BLOCK):
        hi = lo + BLOCK
        d_keys, d_values = part(lo, hi, lo, hi, True)
        if hi < LEN:
            more_keys, more_values = part(lo, hi, hi, LEN, False)
            d_keys += more_keys
            d_values += more_values
        out_ref[1, 0, :, lo:hi] = d_keys.astype(LOW)
        out_ref[2, 0, :, lo:hi] = d_values.astype(LOW)
    d_query = dq_ref[...].astype(LOW).astype(WIDE) * HEAD ** (-0.5)
    out_ref[0, 0] = d_query.astype(LOW)


ANY = pl.BlockSpec(memory_space=pl.ANY)


def kind(which):
    return pl.BlockSpec((1, 1, HEAD, LEN), lambda head: (which, head, 0, 0))


QKV = [kind(0), kind(1), kind(2)]
PER_HEAD = pl.BlockSpec((1, HEAD, LEN), lambda head: (head, 0, 0))
PER_ROW = pl.BlockSpec((1, 1, LEN), lambda head: (head, 0, 0))


def attention(qkv):
    heads = qkv.shape[1]
    return pl.pallas_call(
        attend,
        grid=(heads,),
        in_specs=QKV,
        out_specs=[PER_HEAD, PER_ROW],
        out_shape=[
            jax.ShapeDtypeStruct((heads, HEAD, LEN), LOW),
            jax.ShapeDtypeStruct((heads, 1, LEN), WIDE),
        ],
        compiler_params=pltpu.CompilerParams(vmem_limit_bytes=VMEM),
        cost_estimate=SMALL,
        name="attention",
    )(qkv, qkv, qkv)


def attention_back(qkv, out, d_out, lse, *earlier):
    heads = qkv.shape[1]
    return pl.pallas_call(
        attend_back,
        grid=(heads,),
        in_specs=QKV + [PER_HEAD, PER_HEAD, PER_ROW] + [ANY] * len(earlier),
        out_specs=pl.BlockSpec((3, 1, HEAD, LEN), lambda head: (0, head, 0, 0)),
        out_shape=jax.ShapeDtypeStruct((3, heads, HEAD, LEN), LOW),
        scratch_shapes=[pltpu.VMEM((HEAD, LEN), WIDE)],
        compiler_params=pltpu.CompilerParams(vmem_limit_bytes=VMEM),
        cost_estimate=SMALL,
        name="attention_back",
    )(qkv, qkv, qkv, out, d_out, lse, *earlier)


def bits(size, odd):
    above = [1 << b for b in range(1, size.bit_length() - 1)]
    return above if odd else above[::-1]


def exchanges(size):
    steps = [
        [(d, d ^ (odd if d & 1 else even)) for d in range(size)]
        for even, odd in zip(bits(size, False), bits(size, True))
    ]
    return steps + [[(d, d ^ 1) for d in range(size)]]


def turned(value, size, odd):
    count = size.bit_length() - 2
    back = value * 0
    for b in range(count):
        back = back | (((value >> b) & 1) << (count - 1 - b))
    return jnp.where(odd == 1, value, back)


def slot_of(index, place, size):
    mask = index ^ place
    low = mask & 1
    return low * (size // 2) + turned(mask >> 1, size, (place & 1) ^ low)


def index_of(slot, place, size):
    low = slot // (size // 2)
    return ((turned(slot % (size // 2), size, (place & 1) ^ low) << 1) | low) ^ place


def swap(value, step):
    return lax.ppermute(value, "dp", step)


def add_low(left, right):
    return (left.astype(WIDE) + right.astype(WIDE)).astype(LOW)


def across(piece, mask, size):
    return lax.ppermute(piece, "tensor", [(t, t ^ mask) for t in range(size)])


ORDER = (0, 2, 1, 3)


def to_others(piece, size):
    return [across(piece, m, size) for m in ORDER[1:]]


def nothing(*refs):
    pass


def after(value, *earlier):
    return pl.pallas_call(
        nothing,
        in_specs=[ANY] * (1 + len(earlier)),
        out_specs=ANY,
        out_shape=jax.ShapeDtypeStruct(value.shape, value.dtype),
        input_output_aliases={0: 0},
        cost_estimate=SMALL,
        name="after",
    )(value, *earlier)


def to_right(piece, size):
    return lax.ppermute(piece, "tensor", [(t, (t + 1) % size) for t in range(size)])


def to_left(piece, size):
    return lax.ppermute(piece, "tensor", [(t, (t - 1) % size) for t in range(size)])


def onward(pair, size):
    rows = pair[0].shape[0] // 2
    return to_right(pair[0][:rows], size), to_left(pair[1][rows:], size)


def assemble_near(me_ref, own_ref, left_ref, right_ref, out_ref):
    for step, piece_ref in enumerate((own_ref, left_ref, right_ref)):

        @pl.when(pl.program_id(0) == step)
        def _(piece_ref=piece_ref):
            out_ref[...] = piece_ref[...]


def assemble_far(me_ref, whole_ref, first_ref, second_ref, out_ref):
    rows = first_ref.shape[0]
    out_ref[:rows] = first_ref[...]
    out_ref[rows:] = second_ref[...]


def assembled(own, near, far):
    size = 4
    rows, width = own.shape
    full = pl.BlockSpec((rows, width), lambda g, me: (0, 0))
    part = pl.BlockSpec((rows // 2, width), lambda g, me: (0, 0))

    def turn(g):
        return jnp.where(g == 2, 1, -g)

    shape = jax.ShapeDtypeStruct((size * rows, width), own.dtype)
    me = lax.axis_index("tensor")[None]
    whole = pl.pallas_call(
        assemble_near,
        grid_spec=pltpu.PrefetchScalarGridSpec(
            num_scalar_prefetch=1,
            grid=(3,),
            in_specs=[full, full, full],
            out_specs=pl.BlockSpec(
                (rows, width), lambda g, me: (lax.rem(me[0] + turn(g) + size, size), 0)
            ),
        ),
        out_shape=shape,
        compiler_params=pltpu.CompilerParams(vmem_limit_bytes=VMEM),
        cost_estimate=SMALL,
        name="assemble_near",
    )(me, own, *near)
    return pl.pallas_call(
        assemble_far,
        grid_spec=pltpu.PrefetchScalarGridSpec(
            num_scalar_prefetch=1,
            grid=(1,),
            in_specs=[ANY, part, part],
            out_specs=pl.BlockSpec((rows, width), lambda g, me: (lax.rem(me[0] + 2, size), 0)),
        ),
        out_shape=shape,
        input_output_aliases={1: 0},
        compiler_params=pltpu.CompilerParams(vmem_limit_bytes=VMEM),
        cost_estimate=SMALL,
        name="assemble_far",
    )(me, whole, *far)


def pick(place_ref, in_ref, *refs):
    refs[-1][...] = in_ref[...].reshape(refs[-1].shape).astype(refs[-1].dtype)


def reorder_call(kernel, place, values, earlier, count, in_spec, out_spec, shape, dtype):
    return pl.pallas_call(
        kernel,
        grid_spec=pltpu.PrefetchScalarGridSpec(
            num_scalar_prefetch=1,
            grid=(count,),
            in_specs=[in_spec] * len(values) + [ANY] * len(earlier),
            out_specs=out_spec,
        ),
        out_shape=jax.ShapeDtypeStruct(shape, dtype),
        compiler_params=pltpu.CompilerParams(vmem_limit_bytes=VMEM),
        name="reorder",
    )(place[None], *values, *earlier)


def by_index(slots, place, dtype, *earlier):
    count, rows, width = slots.shape
    return reorder_call(
        pick,
        place,
        [slots],
        earlier,
        count,
        pl.BlockSpec((1, rows, width), lambda j, p: (slot_of(j, p[0], count), 0, 0)),
        pl.BlockSpec((1, rows, width), lambda j, p: (j, 0, 0)),
        slots.shape,
        dtype,
    )


def split_two(place_ref, in_ref, first_ref, second_ref):
    first_ref[0] = in_ref[0, 0].astype(first_ref.dtype)
    second_ref[0] = in_ref[1, 0].astype(second_ref.dtype)


def two_by_index(slots, place):
    _, count, rows, width = slots.shape
    one = pl.BlockSpec((1, rows, width), lambda j, p: (j, 0, 0))
    shape = (count, rows, width)
    return pl.pallas_call(
        split_two,
        grid_spec=pltpu.PrefetchScalarGridSpec(
            num_scalar_prefetch=1,
            grid=(count,),
            in_specs=[
                pl.BlockSpec((2, 1, rows, width), lambda j, p: (0, slot_of(j, p[0], count), 0, 0))
            ],
            out_specs=[one, one],
        ),
        out_shape=[jax.ShapeDtypeStruct(shape, LOW), jax.ShapeDtypeStruct(shape, WIDE)],
        compiler_params=pltpu.CompilerParams(vmem_limit_bytes=VMEM),
        name="reorder",
    )(place[None], slots)


def groups_by_index(slots, place):
    count, groups, rows, width = slots.shape
    return reorder_call(
        pick,
        place,
        [slots],
        (),
        count,
        pl.BlockSpec((1, groups, rows, width), lambda j, p: (slot_of(j, p[0], count), 0, 0, 0)),
        pl.BlockSpec((groups, 1, rows, width), lambda j, p: (0, j, 0, 0)),
        (groups, count, rows, width),
        LOW,
    )


def groups_by_slot(values, place, *earlier):
    groups, count, rows, width = values.shape
    return reorder_call(
        pick,
        place,
        [values],
        earlier,
        count,
        pl.BlockSpec((groups, 1, rows, width), lambda k, p: (0, index_of(k, p[0], count), 0, 0)),
        pl.BlockSpec((1, groups, rows, width), lambda k, p: (k, 0, 0, 0)),
        (count, groups, rows, width),
        LOW,
    )


def middle(
    attn_ref, w_out_ref, x_ref, dy_ref, rows_ref, w_ref, bias_ref,
    out_ref, mine_ref, theirs_ref, resid_ref, dw_out_ref, sums_ref, dw_ref, db_ref,
    a_ref, normed_ref, rstd_ref, mixed_ref, da_ref,
):
    @pl.when(pl.program_id(0) == 0)
    def _():
        resid = x_ref[...].astype(WIDE) + dot(attn_ref[...], w_out_ref[...], TN) + rows_ref[0:1]
        normed, rstd = norm_parts(resid)
        resid_ref[...] = resid
        normed_ref[...] = normed
        rstd_ref[...] = rstd
        a_ref[...] = (normed * rows_ref[1:2] + rows_ref[2:3]).astype(LOW)
        mixed_ref[...] = jnp.zeros_like(mixed_ref)
        da_ref[...] = jnp.zeros_like(da_ref)

    a_second, dy = a_ref[...], dy_ref[...]
    actives, d_uppers = [], []
    for lo in range(0, UNITS, BLOCK):
        some = slice(lo, lo + BLOCK)
        upper = dot(a_second, w_ref[0, some], NT) + bias_ref[:, some]
        square = upper * upper
        curve = jnp.tanh(0.7978845608028654 * (upper + 0.044715 * upper * square))
        rise = 0.5 * (1.0 + curve)
        active = (upper * rise).astype(LOW)
        slope = rise + 0.5 * upper * (1.0 - curve * curve) * (
            0.7978845608028654 * (1.0 + 3.0 * 0.044715 * square)
        )
        d_upper = dot(dy, w_ref[1, some], NT) * slope
        db_ref[:, some] = jnp.sum(d_upper, axis=0, keepdims=True)
        actives.append(active)
        d_uppers.append(d_upper.astype(LOW))
    active = jnp.concatenate(actives, axis=1)
    d_upper = jnp.concatenate(d_uppers, axis=1)
    mixed_ref[...] += dot(active, w_ref[1])
    da_ref[...] += dot(d_upper, w_ref[0])
    rows = dw_ref.shape[2]
    dw_ref[:, 0] = dot(d_upper, a_second, TN).astype(LOW).reshape(-1, rows, dw_ref.shape[3])
    dw_ref[:, 1] = dot(active, dy, TN).astype(LOW).reshape(-1, rows, dw_ref.shape[3])

    @pl.when(pl.program_id(0) == pl.num_programs(0) - 1)
    def _():
        out_ref[...] = (resid_ref[...] + mixed_ref[...] + rows_ref[3:4]).astype(LOW)
        d_resid, d_gain, d_bias = norm_back(
            normed_ref[...], rstd_ref[...], rows_ref[1:2], da_ref[...]
        )
        dy_wide = dy_ref[...].astype(WIDE)
        d_resid += dy_wide
        resid_ref[...] = d_resid
        sums_ref[0:1] = d_gain[None]
        sums_ref[1:2] = d_bias[None]
        sums_ref[2:3] = jnp.sum(d_resid, axis=0, keepdims=True)
        sums_ref[3:4] = jnp.sum(dy_wide, axis=0, keepdims=True)
        sums_ref[4:8] = jnp.zeros_like(sums_ref[4:8])
        low = d_resid.astype(LOW)
        split = mine_ref.shape[0]
        mine_ref[...] = dot(w_out_ref[:split], low, NT).astype(LOW)
        theirs_ref[...] = dot(w_out_ref[split:], low, NT).astype(LOW)
        dw_out_ref[...] = dot(attn_ref[...], low).astype(LOW)


def middle_call(attn, w_out, x, dy, rows, weights, bias, parts):
    tokens, width = x.shape
    hidden = weights.shape[1]
    once = pl.Buffered(1)

    def whole(*shape):
        return pl.BlockSpec(shape, lambda g: (0,) * len(shape), pipeline_mode=once)

    some = pl.BlockSpec((2, UNITS, width), lambda g: (0, g, 0))
    each = hidden // parts
    slots = pl.BlockSpec((UNITS // each, 2, each, width), lambda g: (g, 0, 0, 0))
    row = pl.BlockSpec((1, UNITS), lambda g: (0, g))
    local = attn.shape[0] // 2
    return pl.pallas_call(
        middle,
        grid=(hidden // UNITS,),
        in_specs=[
            whole(*attn.shape),
            whole(*w_out.shape),
            whole(tokens, width),
            whole(tokens, width),
            whole(*rows.shape),
            some,
            row,
        ],
        out_specs=[
            whole(tokens, width),
            whole(local, tokens),
            whole(local, tokens),
            whole(tokens, width),
            whole(*w_out.shape),
            whole(8, width),
            slots,
            row,
        ],
        out_shape=[
            jax.ShapeDtypeStruct((tokens, width), LOW),
            jax.ShapeDtypeStruct((local, tokens), LOW),
            jax.ShapeDtypeStruct((local, tokens), LOW),
            jax.ShapeDtypeStruct((tokens, width), WIDE),
            jax.ShapeDtypeStruct(w_out.shape, LOW),
            jax.ShapeDtypeStruct((8, width), WIDE),
            jax.ShapeDtypeStruct((parts, 2, each, width), LOW),
            jax.ShapeDtypeStruct((1, hidden), WIDE),
        ],
        scratch_shapes=[
            pltpu.VMEM((tokens, width), LOW),
            pltpu.VMEM((tokens, width), WIDE),
            pltpu.VMEM((tokens, 1), WIDE),
            pltpu.VMEM((tokens, width), WIDE),
            pltpu.VMEM((tokens, width), WIDE),
        ],
        compiler_params=pltpu.CompilerParams(vmem_limit_bytes=48 * 2**20),
        cost_estimate=SMALL,
        name="middle",
    )(attn, w_out, x, dy, rows, weights, bias)


def first_back(half_ref, d_a_ref, d_b_ref, w_a_ref, w_b_ref, *refs):
    mine_ref, theirs_ref = refs[-2:]
    own = mine_ref.shape[0]
    for out_ref, which in ((theirs_ref, 1 - half_ref[0]), (mine_ref, half_ref[0])):
        some = pl.ds(pl.multiple_of(which * own, own), own)
        value = dot(d_a_ref[:, some], w_a_ref[...], TN) + dot(d_b_ref[:, some], w_b_ref[...], TN)
        out_ref[...] = value.astype(out_ref.dtype)


def first_back_call(half, d_a, d_b, w_a, w_b, own, *earlier):
    width = w_a.shape[1]

    def whole(*shape):
        return pl.BlockSpec(shape, lambda g, h: (0,) * len(shape))

    return pl.pallas_call(
        first_back,
        grid_spec=pltpu.PrefetchScalarGridSpec(
            num_scalar_prefetch=1,
            grid=(1,),
            in_specs=[whole(*v.shape) for v in (d_a, d_b, w_a, w_b)] + [ANY] * len(earlier),
            out_specs=[whole(own, width), whole(own, width)],
        ),
        out_shape=[
            jax.ShapeDtypeStruct((own, width), WIDE),
            jax.ShapeDtypeStruct((own, width), LOW),
        ],
        compiler_params=pltpu.CompilerParams(vmem_limit_bytes=VMEM),
        cost_estimate=SMALL,
        name="first_back",
    )(half[None], d_a, d_b, w_a, w_b, *earlier)


def weight_back(place_ref, a_ref, d_a_ref, d_b_ref, *refs):
    refs[-1][0, 0] = dot(d_a_ref[0], a_ref[...]).astype(LOW)
    refs[-1][0, 1] = dot(d_b_ref[0], a_ref[...]).astype(LOW)


def weight_back_call(place, a_first, d_a, d_b, *earlier):
    count, rows, tokens = d_a.shape
    width = a_first.shape[1]
    piece = pl.BlockSpec((1, rows, tokens), lambda k, p: (index_of(k, p[0], count), 0, 0))
    return pl.pallas_call(
        weight_back,
        grid_spec=pltpu.PrefetchScalarGridSpec(
            num_scalar_prefetch=1,
            grid=(count,),
            in_specs=[pl.BlockSpec((tokens, width), lambda k, p: (0, 0)), piece, piece]
            + [ANY] * len(earlier),
            out_specs=pl.BlockSpec((1, 2, rows, width), lambda k, p: (k, 0, 0, 0)),
        ),
        out_shape=jax.ShapeDtypeStruct((count, 2, rows, width), LOW),
        compiler_params=pltpu.CompilerParams(vmem_limit_bytes=VMEM),
        cost_estimate=SMALL,
        name="weight_back",
    )(place[None], a_first, d_a, d_b, *earlier)


def shards(
    inputs,
    gain1,
    bias1,
    w_qkv,
    bias_q,
    bias_v,
    w_out,
    bias_out,
    gain2,
    bias2,
    w_fc,
    bias_fc,
    w_proj,
    bias_proj,
    cotangent,
):
    n_dp, n_t = lax.axis_size("dp"), lax.axis_size("tensor")
    place, me = lax.axis_index("dp"), lax.axis_index("tensor")
    count, width = inputs.shape
    local = w_qkv.shape[2]
    hidden = w_fc.shape[1]
    heads = local // HEAD
    scale = HEAD ** (-0.5)
    own = count // n_t
    half = lax.rem(me, 2)
    rows_q, rows_o, rows_f = 3 * local // n_dp, local // n_dp, hidden // n_dp

    plane = exchanges(n_dp)
    near, last = plane[:-1], plane[-1]

    qkv_own = w_qkv.transpose(1, 2, 0).reshape(3 * local, width)
    q = across(lax.dynamic_slice_in_dim(qkv_own, place * rows_q, rows_q, 0), 2, n_t)
    vector = across(jnp.concatenate([bias_q, bias_v, bias_fc]), 2, n_t)
    biases = [bias_fc, vector[2 * local :], across(bias_fc, 1, n_t), across(bias_fc, 3, n_t)]
    o = lax.dynamic_slice_in_dim(w_out, place * rows_o, rows_o, 0)
    o_parts = to_others(o, n_t)
    w = jnp.stack(
        [
            lax.dynamic_slice_in_dim(w_fc, place * rows_f, rows_f, 1).T,
            lax.dynamic_slice_in_dim(w_proj, place * rows_f, rows_f, 0),
        ]
    )
    w = lax.all_gather(w, ("dp", "tensor"), axis=1, tiled=True)

    x_seq = lax.dynamic_slice_in_dim(inputs, (me // 2) * LEN, LEN, 0).astype(WIDE)
    normed, _ = norm_parts(x_seq)
    a_first = (normed * gain1 + bias1).astype(LOW)

    def project(weight, add_q, add_v):
        proj = dot(weight, a_first, NT)
        query = (proj[:local] + add_q[:, None]) * scale
        values = proj[2 * local :] + add_v[:, None]
        proj = jnp.concatenate([query, proj[local : 2 * local], values], axis=0)
        return proj.astype(LOW).reshape(3, heads, HEAD, LEN)

    def halves(value):
        mine = lax.dynamic_slice_in_dim(value, half * own, own, value.ndim - 1)
        theirs = lax.dynamic_slice_in_dim(value, (1 - half) * own, own, value.ndim - 1)
        return mine, theirs

    def both(held, step, axis=0):
        return jnp.concatenate([held, swap(held, step)], axis=axis)

    q, o = q[None], jnp.stack([o] + o_parts)[None]
    for step in near:
        q = both(q, step)
    q_take = swap(q, last)
    proj_a = project(qkv_own, bias_q, bias_v)
    out_a, lse_a = attention(proj_a)
    mine_a, theirs_a = halves(out_a.reshape(local, LEN))
    theirs_a = across(theirs_a, 1, n_t)
    for step in plane:
        o = both(o, step)
    qkv_other = by_index(jnp.concatenate([q, q_take], axis=0), place, LOW)
    qkv_other = qkv_other.reshape(3 * local, width)
    proj_b = project(qkv_other, vector[:local], vector[local : 2 * local])
    out_b, lse_b = attention(proj_b)
    mine_b, theirs_b = halves(out_b.reshape(local, LEN))
    theirs_b = across(theirs_b, 1, n_t)
    w_out_all = groups_by_index(o, place).reshape(n_t * local, width)
    attn_low = jnp.concatenate([mine_a, mine_b, theirs_a, theirs_b], axis=0)
    place_of = jnp.array([ORDER.index(m) for m in range(n_t)], jnp.int32)
    place_of = place_of[jnp.arange(n_t, dtype=jnp.int32) ^ me]
    bias_fc_all = jnp.stack(biases).reshape(n_t, n_dp, rows_f)
    bias_fc_all = bias_fc_all.at[place_of].get(mode="promise_in_bounds")
    bias_fc_all = bias_fc_all.transpose(1, 0, 2).reshape(1, n_t * hidden)

    x_own = lax.dynamic_slice_in_dim(inputs, me * own, own, 0)
    dy = lax.dynamic_slice_in_dim(cotangent, me * own, own, 0)
    rows = jnp.stack([bias_out, gain2, bias2, bias_proj])
    output, d_mine, d_theirs, d_resid, o, sums_row, w, sums_fc = middle_call(
        attn_low, w_out_all, x_own, dy, rows, w, bias_fc_all, n_dp
    )
    from_left = to_right(output, n_t)
    d_take = across(d_theirs, 1, n_t)
    output_near = (from_left, to_left(after(output, d_take), n_t))

    def parted(held, axis=0):
        middle = held.shape[axis] // 2
        return jnp.split(held, [middle], axis=axis)

    def folded(held, taken, axis=0):
        held, taken = parted(held, axis), parted(taken, axis)
        return add_low(held[0], taken[0]), add_low(held[1], taken[1])

    w = lax.psum_scatter(w, "dp")
    d_out = jnp.where(
        half == 0,
        jnp.concatenate([d_mine, d_take], axis=1),
        jnp.concatenate([d_take, d_mine], axis=1),
    )
    d_out = d_out.reshape(2, heads, HEAD, LEN)

    down = near[::-1]
    d_proj_a = attention_back(proj_a, out_a, d_out[0], lse_a)
    d_proj_b = attention_back(proj_b, out_b, d_out[1], lse_b, d_proj_a)
    d_proj_a = d_proj_a.reshape(3 * local, LEN)
    d_proj_b = d_proj_b.reshape(3 * local, LEN)

    d_first, d_theirs = first_back_call(
        half, d_proj_a, d_proj_b, qkv_own, qkv_other, own, *output_near
    )
    d_first_take = across(d_theirs, 1, n_t)
    output_near = tuple(after(part, d_first_take) for part in output_near)
    output_far = onward(output_near, n_t)
    sums_a = jnp.sum(d_proj_a.reshape(3, local, LEN).astype(WIDE), axis=2)
    sums_b = jnp.sum(d_proj_b.reshape(3, local, LEN).astype(WIDE), axis=2)
    group = jnp.arange(n_t, dtype=jnp.int32)[None, :, None]
    bias_rows = jnp.where(group == me, sums_a[:, None], 0.0)
    bias_rows += jnp.where(group == (me ^ 2), sums_b[:, None], 0.0)
    sums_fc = after(sums_fc, d_first_take).reshape(n_dp, n_t, rows_f).transpose(1, 0, 2)
    w = w.reshape(2, n_t, rows_f, width)
    w = [lax.dynamic_index_in_dim(w, me ^ m, 1, keepdims=False) for m in ORDER]
    w_parts = [across(w[at], m, n_t) for at, m in enumerate(ORDER) if at]
    normed1, rstd1 = norm_parts(x_own.astype(WIDE))
    d_first = d_first + d_first_take.astype(WIDE)
    d_in_norm, d_gain1, d_bias1 = norm_back(normed1, rstd1, gain1, d_first)
    d_inputs = (d_resid + d_in_norm).astype(LOW)
    inputs_near = to_right(d_inputs, n_t), to_left(d_inputs, n_t)

    d_proj_a, d_proj_b = (d.reshape(n_dp, rows_q, LEN) for d in (d_proj_a, d_proj_b))
    q, q_send = parted(weight_back_call(place, a_first, d_proj_a, d_proj_b, d_inputs))
    q_take = swap(q_send, last)
    o, o_send = parted(groups_by_slot(o.reshape(n_t, n_dp, rows_o, width), place, d_inputs))
    o_take = swap(o_send, last)
    for step in down:
        q, q_send = folded(q, q_take)
        q_take = swap(q_send, step)
        o, o_send = folded(o, o_take)
        o_take = swap(o_send, step)

    def sum_tensor(held):
        return held[0], [across(held[at], m, n_t) for at, m in enumerate(ORDER) if at]

    def total_of(mine, parts):
        total = mine.astype(WIDE)
        for part in parts:
            total += part.astype(WIDE)
        return total.astype(LOW)

    w_parts[0] = after(w_parts[0], *output_far, *inputs_near)
    w = total_of(w[0], w_parts)[:, None]
    inputs_far = onward(inputs_near, n_t)
    o, o_parts = sum_tensor(add_low(o, after(o_take, w))[0])
    q = add_low(q, after(q_take, w))[0]
    q_take = across(q[1], 2, n_t)
    vectors = jnp.concatenate(
        [
            d_gain1,
            d_bias1,
            sums_row[:4].reshape(-1),
            bias_rows[0].reshape(-1),
            bias_rows[2].reshape(-1),
            sums_fc.reshape(-1),
        ]
    ).reshape(-1, 128)
    vectors = after(vectors, d_inputs)
    for step in plane:
        vectors = vectors + swap(vectors, step)
    vectors = after(vectors, w)
    vectors = vectors + across(vectors, 1, n_t)
    vectors = after(vectors, *inputs_far)
    vectors = vectors + across(vectors, 2, n_t)
    o = total_of(o, o_parts)[None]
    q = add_low(q[0], q_take)[None]
    for step in plane:
        o, q = both(o, step), both(q, step)
    for step in plane:
        w = both(w, step, 1)
    d_w_out = by_index(o, place, WIDE).reshape(local, width)
    d_w_qkv = by_index(q, place, WIDE).reshape(3, local, width).transpose(2, 0, 1)
    whole_output = assembled(output, output_near, output_far)
    whole_d_inputs = assembled(d_inputs, inputs_near, inputs_far)
    d_w_fc, d_w_proj = two_by_index(w, place)
    d_w_proj = d_w_proj.reshape(hidden, width)
    d_w_fc = d_w_fc.reshape(hidden, width).T.astype(WIDE)
    vectors = vectors.reshape(-1, width)
    d_gain1, d_bias1, d_gain2, d_bias2, d_bias_out, d_bias_proj = (vectors[r] for r in range(6))
    d_bias_q = lax.dynamic_slice_in_dim(vectors[6], me * local, local, 0)
    d_bias_v = lax.dynamic_slice_in_dim(vectors[7], me * local, local, 0)
    d_bias_fc = lax.dynamic_slice_in_dim(vectors[8:].reshape(-1), me * hidden, hidden, 0)
    return (
        whole_output,
        whole_d_inputs,
        d_gain1,
        d_bias1,
        d_w_qkv,
        d_bias_q,
        d_bias_v,
        d_w_out,
        d_bias_out,
        d_gain2,
        d_bias2,
        d_w_fc,
        d_bias_fc,
        d_w_proj,
        d_bias_proj,
    )


def solution(mesh):
    placed = (
        P("dp", None),
        P(),
        P(),
        P(None, None, "tensor"),
        P("tensor"),
        P("tensor"),
        P("tensor", None),
        P(),
        P(),
        P(),
        P(None, "tensor"),
        P("tensor"),
        P("tensor", None),
        P(),
        P("dp", None),
    )
    return jax.shard_map(
        shards,
        mesh=mesh,
        in_specs=placed,
        out_specs=(
            P("dp", None),
            P("dp", None),
            P(),
            P(),
            P(None, None, "tensor"),
            P("tensor"),
            P("tensor"),
            P("tensor", None),
            P(),
            P(),
            P(),
            P(None, "tensor"),
            P("tensor"),
            P("tensor", None),
            P(),
        ),
        check_vma=False,
    )
```

```python
import jax
import jax.numpy as jnp
from jax import lax
from jax.experimental import pallas as pl
from jax.experimental.pallas import tpu as pltpu
from jax.sharding import PartitionSpec as P

HEAD = 64
LEN = 1024
BLOCK = 256
UNITS = 768
VMEM = 32 * 2**20
SMALL = pl.CostEstimate(flops=1, bytes_accessed=1, transcendentals=0)


LOW = jnp.bfloat16
WIDE = jnp.float32

NN = (((1,), (0,)), ((), ()))
NT = (((1,), (1,)), ((), ()))
TN = (((0,), (0,)), ((), ()))
TT = (((0,), (1,)), ((), ()))


def dot(left, right, dims=NN):
    return lax.dot_general(left, right, dims, preferred_element_type=WIDE)


def norm_parts(value):
    centre = value - jnp.mean(value, axis=-1, keepdims=True)
    rstd = lax.rsqrt(jnp.mean(centre * centre, axis=-1, keepdims=True) + 1e-05)
    return (centre * rstd, rstd)


def norm_back(normed, rstd, gain, grad):
    scaled = grad * gain
    inner = (
        scaled
        - jnp.mean(scaled, axis=-1, keepdims=True)
        - normed * jnp.mean(scaled * normed, axis=-1, keepdims=True)
    )
    return (rstd * inner, jnp.sum(grad * normed, axis=0), jnp.sum(grad, axis=0))


def causal(scores):
    keys = lax.broadcasted_iota(jnp.int32, scores.shape, 0)
    queries = lax.broadcasted_iota(jnp.int32, scores.shape, 1)
    return keys <= queries


def attend(q_ref, k_ref, v_ref, o_ref, lse_ref):
    query, values = q_ref[0, 0], v_ref[0, 0]
    keys = k_ref[0, 0].T
    for lo in range(0, LEN, BLOCK):
        hi = lo + BLOCK
        near = dot(keys[lo:hi], query[:, lo:hi])
        near = jnp.where(causal(near), near, -1e30)
        top = jnp.max(near, axis=0, keepdims=True)
        if lo:
            far = dot(keys[:lo], query[:, lo:hi])
            top = jnp.maximum(top, jnp.max(far, axis=0, keepdims=True))
        near = jnp.exp(near - top)
        total = jnp.sum(near, axis=0, keepdims=True)
        out = dot(values[:, lo:hi], near.astype(LOW))
        if lo:
            far = jnp.exp(far - top)
            total += jnp.sum(far, axis=0, keepdims=True)
            out += dot(values[:, :lo], far.astype(LOW))
        o_ref[0, :, lo:hi] = (out / total).astype(LOW)
        lse_ref[0, :, lo:hi] = top + jnp.log(total)


def attend_back(q_ref, k_ref, v_ref, o_ref, do_ref, lse_ref, *refs):
    out_ref, dq_ref = refs[-2:]
    query, keys_t, d_out = q_ref[0, 0], k_ref[0, 0], do_ref[0]
    keys, values = keys_t.T, v_ref[0, 0].T
    lse = lse_ref[0]
    delta = jnp.sum(d_out.astype(WIDE) * o_ref[0].astype(WIDE), axis=0, keepdims=True)

    def part(lo, hi, begin, end, mask):
        probs = jnp.exp(dot(keys[lo:hi], query[:, begin:end]) - lse[:, begin:end])
        if mask:
            probs = jnp.where(causal(probs), probs, 0.0)
        d_probs = dot(values[lo:hi], d_out[:, begin:end])
        d_scores = (probs * (d_probs - delta[:, begin:end])).astype(LOW)
        d_values = dot(d_out[:, begin:end], probs.astype(LOW), NT)
        d_keys = dot(query[:, begin:end], d_scores, NT)
        d_query = dot(keys_t[:, lo:hi], d_scores)
        if lo == 0:
            dq_ref[:, begin:end] = d_query
        else:
            dq_ref[:, begin:end] += d_query
        return d_keys, d_values

    for lo in range(0, LEN, BLOCK):
        hi = lo + BLOCK
        d_keys, d_values = part(lo, hi, lo, hi, True)
        if hi < LEN:
            more_keys, more_values = part(lo, hi, hi, LEN, False)
            d_keys += more_keys
            d_values += more_values
        out_ref[1, 0, :, lo:hi] = d_keys.astype(LOW)
        out_ref[2, 0, :, lo:hi] = d_values.astype(LOW)
    d_query = dq_ref[...].astype(LOW).astype(WIDE) * HEAD ** (-0.5)
    out_ref[0, 0] = d_query.astype(LOW)


ANY = pl.BlockSpec(memory_space=pl.ANY)


def kind(which):
    return pl.BlockSpec((1, 1, HEAD, LEN), lambda head: (which, head, 0, 0))


QKV = [kind(0), kind(1), kind(2)]
PER_HEAD = pl.BlockSpec((1, HEAD, LEN), lambda head: (head, 0, 0))
PER_ROW = pl.BlockSpec((1, 1, LEN), lambda head: (head, 0, 0))


def attention(qkv):
    heads = qkv.shape[1]
    return pl.pallas_call(
        attend,
        grid=(heads,),
        in_specs=QKV,
        out_specs=[PER_HEAD, PER_ROW],
        out_shape=[
            jax.ShapeDtypeStruct((heads, HEAD, LEN), LOW),
            jax.ShapeDtypeStruct((heads, 1, LEN), WIDE),
        ],
        compiler_params=pltpu.CompilerParams(vmem_limit_bytes=VMEM),
        cost_estimate=SMALL,
        name="attention",
    )(qkv, qkv, qkv)


def attention_back(qkv, out, d_out, lse, *earlier):
    heads = qkv.shape[1]
    return pl.pallas_call(
        attend_back,
        grid=(heads,),
        in_specs=QKV + [PER_HEAD, PER_HEAD, PER_ROW] + [ANY] * len(earlier),
        out_specs=pl.BlockSpec((3, 1, HEAD, LEN), lambda head: (0, head, 0, 0)),
        out_shape=jax.ShapeDtypeStruct((3, heads, HEAD, LEN), LOW),
        scratch_shapes=[pltpu.VMEM((HEAD, LEN), WIDE)],
        compiler_params=pltpu.CompilerParams(vmem_limit_bytes=VMEM),
        cost_estimate=SMALL,
        name="attention_back",
    )(qkv, qkv, qkv, out, d_out, lse, *earlier)


def bits(size, odd):
    above = [1 << b for b in range(1, size.bit_length() - 1)]
    return above if odd else above[::-1]


def exchanges(size):
    steps = [
        [(d, d ^ (odd if d & 1 else even)) for d in range(size)]
        for even, odd in zip(bits(size, False), bits(size, True))
    ]
    return steps + [[(d, d ^ 1) for d in range(size)]]


def turned(value, size, odd):
    count = size.bit_length() - 2
    back = value * 0
    for b in range(count):
        back = back | (((value >> b) & 1) << (count - 1 - b))
    return jnp.where(odd == 1, value, back)


def slot_of(index, place, size):
    mask = index ^ place
    low = mask & 1
    return low * (size // 2) + turned(mask >> 1, size, (place & 1) ^ low)


def index_of(slot, place, size):
    low = slot // (size // 2)
    return ((turned(slot % (size // 2), size, (place & 1) ^ low) << 1) | low) ^ place


def swap(value, step):
    return lax.ppermute(value, "dp", step)


def add_low(left, right):
    return (left.astype(WIDE) + right.astype(WIDE)).astype(LOW)


def across(piece, mask, size):
    return lax.ppermute(piece, "tensor", [(t, t ^ mask) for t in range(size)])


ORDER = (0, 2, 1, 3)


def to_others(piece, size):
    return [across(piece, m, size) for m in ORDER[1:]]


def nothing(*refs):
    pass


def after(value, *earlier):
    return pl.pallas_call(
        nothing,
        in_specs=[ANY] * (1 + len(earlier)),
        out_specs=ANY,
        out_shape=jax.ShapeDtypeStruct(value.shape, value.dtype),
        input_output_aliases={0: 0},
        cost_estimate=SMALL,
        name="after",
    )(value, *earlier)


def to_right(piece, size):
    return lax.ppermute(piece, "tensor", [(t, (t + 1) % size) for t in range(size)])


def to_left(piece, size):
    return lax.ppermute(piece, "tensor", [(t, (t - 1) % size) for t in range(size)])


def onward(pair, size):
    rows = pair[0].shape[0] // 2
    return to_right(pair[0][:rows], size), to_left(pair[1][rows:], size)


def assemble_near(me_ref, own_ref, left_ref, right_ref, out_ref):
    for step, piece_ref in enumerate((own_ref, left_ref, right_ref)):

        @pl.when(pl.program_id(0) == step)
        def _(piece_ref=piece_ref):
            out_ref[...] = piece_ref[...]


def assemble_far(me_ref, whole_ref, first_ref, second_ref, out_ref):
    rows = first_ref.shape[0]
    out_ref[:rows] = first_ref[...]
    out_ref[rows:] = second_ref[...]


def assembled(own, near, far):
    size = 4
    rows, width = own.shape
    full = pl.BlockSpec((rows, width), lambda g, me: (0, 0))
    part = pl.BlockSpec((rows // 2, width), lambda g, me: (0, 0))

    def turn(g):
        return jnp.where(g == 2, 1, -g)

    shape = jax.ShapeDtypeStruct((size * rows, width), own.dtype)
    me = lax.axis_index("tensor")[None]
    whole = pl.pallas_call(
        assemble_near,
        grid_spec=pltpu.PrefetchScalarGridSpec(
            num_scalar_prefetch=1,
            grid=(3,),
            in_specs=[full, full, full],
            out_specs=pl.BlockSpec(
                (rows, width), lambda g, me: (lax.rem(me[0] + turn(g) + size, size), 0)
            ),
        ),
        out_shape=shape,
        compiler_params=pltpu.CompilerParams(vmem_limit_bytes=VMEM),
        cost_estimate=SMALL,
        name="assemble_near",
    )(me, own, *near)
    return pl.pallas_call(
        assemble_far,
        grid_spec=pltpu.PrefetchScalarGridSpec(
            num_scalar_prefetch=1,
            grid=(1,),
            in_specs=[ANY, part, part],
            out_specs=pl.BlockSpec((rows, width), lambda g, me: (lax.rem(me[0] + 2, size), 0)),
        ),
        out_shape=shape,
        input_output_aliases={1: 0},
        compiler_params=pltpu.CompilerParams(vmem_limit_bytes=VMEM),
        cost_estimate=SMALL,
        name="assemble_far",
    )(me, whole, *far)


def pick(place_ref, in_ref, *refs):
    refs[-1][...] = in_ref[...].reshape(refs[-1].shape).astype(refs[-1].dtype)


def reorder_call(kernel, place, values, earlier, count, in_spec, out_spec, shape, dtype):
    return pl.pallas_call(
        kernel,
        grid_spec=pltpu.PrefetchScalarGridSpec(
            num_scalar_prefetch=1,
            grid=(count,),
            in_specs=[in_spec] * len(values) + [ANY] * len(earlier),
            out_specs=out_spec,
        ),
        out_shape=jax.ShapeDtypeStruct(shape, dtype),
        compiler_params=pltpu.CompilerParams(vmem_limit_bytes=VMEM),
        name="reorder",
    )(place[None], *values, *earlier)


def by_index(slots, place, dtype, *earlier):
    count, rows, width = slots.shape
    return reorder_call(
        pick,
        place,
        [slots],
        earlier,
        count,
        pl.BlockSpec((1, rows, width), lambda j, p: (slot_of(j, p[0], count), 0, 0)),
        pl.BlockSpec((1, rows, width), lambda j, p: (j, 0, 0)),
        slots.shape,
        dtype,
    )


def split_two(place_ref, in_ref, first_ref, second_ref):
    first_ref[0] = in_ref[0, 0].astype(first_ref.dtype)
    second_ref[0] = in_ref[1, 0].astype(second_ref.dtype)


def two_by_index(slots, place):
    _, count, rows, width = slots.shape
    one = pl.BlockSpec((1, rows, width), lambda j, p: (j, 0, 0))
    shape = (count, rows, width)
    return pl.pallas_call(
        split_two,
        grid_spec=pltpu.PrefetchScalarGridSpec(
            num_scalar_prefetch=1,
            grid=(count,),
            in_specs=[
                pl.BlockSpec((2, 1, rows, width), lambda j, p: (0, slot_of(j, p[0], count), 0, 0))
            ],
            out_specs=[one, one],
        ),
        out_shape=[jax.ShapeDtypeStruct(shape, LOW), jax.ShapeDtypeStruct(shape, WIDE)],
        compiler_params=pltpu.CompilerParams(vmem_limit_bytes=VMEM),
        name="reorder",
    )(place[None], slots)


def turn_two(place_ref, *refs):
    first_ref, second_ref = refs[-2:]
    pieces = [ref[:, 0].astype(WIDE) for ref in refs[:-2]]
    first_ref[...] = jnp.concatenate([piece[0] for piece in pieces], axis=0).T
    second_ref[...] = jnp.concatenate([piece[1] for piece in pieces], axis=0)


def turned_by_index(slots, place):
    _, count, rows, width = slots.shape
    if 4 * rows % 128:
        first, second = two_by_index(slots, place)
        first = first.reshape(count * rows, width).T.astype(WIDE)
        return first, second.reshape(count * rows, width)

    def piece(at):
        return pl.BlockSpec(
            (2, 1, rows, width), lambda g, p: (0, slot_of(4 * g + at, p[0], count), 0, 0)
        )

    return pl.pallas_call(
        turn_two,
        grid_spec=pltpu.PrefetchScalarGridSpec(
            num_scalar_prefetch=1,
            grid=(count // 4,),
            in_specs=[piece(at) for at in range(4)],
            out_specs=[
                pl.BlockSpec((width, 4 * rows), lambda g, p: (0, g)),
                pl.BlockSpec((4 * rows, width), lambda g, p: (g, 0)),
            ],
        ),
        out_shape=[
            jax.ShapeDtypeStruct((width, count * rows), WIDE),
            jax.ShapeDtypeStruct((count * rows, width), WIDE),
        ],
        compiler_params=pltpu.CompilerParams(vmem_limit_bytes=VMEM),
        cost_estimate=SMALL,
        name="reorder",
    )(place[None], slots, slots, slots, slots)


def groups_by_index(slots, place):
    count, groups, rows, width = slots.shape
    return reorder_call(
        pick,
        place,
        [slots],
        (),
        count,
        pl.BlockSpec((1, groups, rows, width), lambda j, p: (slot_of(j, p[0], count), 0, 0, 0)),
        pl.BlockSpec((groups, 1, rows, width), lambda j, p: (0, j, 0, 0)),
        (groups, count, rows, width),
        LOW,
    )


def groups_by_slot(values, place, *earlier):
    groups, count, rows, width = values.shape
    return reorder_call(
        pick,
        place,
        [values],
        earlier,
        count,
        pl.BlockSpec((groups, 1, rows, width), lambda k, p: (0, index_of(k, p[0], count), 0, 0)),
        pl.BlockSpec((1, groups, rows, width), lambda k, p: (k, 0, 0, 0)),
        (count, groups, rows, width),
        LOW,
    )


def middle(
    attn_ref, w_out_ref, x_ref, dy_ref, rows_ref, w_ref, bias_ref,
    out_ref, mine_ref, theirs_ref, resid_ref, dw_out_ref, sums_ref, dw_ref, db_ref,
    a_ref, normed_ref, rstd_ref, mixed_ref, da_ref,
):
    @pl.when(pl.program_id(0) == 0)
    def _():
        resid = x_ref[...].astype(WIDE) + dot(attn_ref[...], w_out_ref[...], TN) + rows_ref[0:1]
        normed, rstd = norm_parts(resid)
        resid_ref[...] = resid
        normed_ref[...] = normed
        rstd_ref[...] = rstd
        a_ref[...] = (normed * rows_ref[1:2] + rows_ref[2:3]).astype(LOW)
        mixed_ref[...] = jnp.zeros_like(mixed_ref)
        da_ref[...] = jnp.zeros_like(da_ref)

    a_second, dy = a_ref[...], dy_ref[...]
    actives, d_uppers = [], []
    for lo in range(0, UNITS, BLOCK):
        some = slice(lo, lo + BLOCK)
        upper = dot(a_second, w_ref[0, some], NT) + bias_ref[:, some]
        square = upper * upper
        curve = jnp.tanh(0.7978845608028654 * (upper + 0.044715 * upper * square))
        rise = 0.5 * (1.0 + curve)
        active = (upper * rise).astype(LOW)
        slope = rise + 0.5 * upper * (1.0 - curve * curve) * (
            0.7978845608028654 * (1.0 + 3.0 * 0.044715 * square)
        )
        d_upper = dot(dy, w_ref[1, some], NT) * slope
        db_ref[:, some] = jnp.sum(d_upper, axis=0, keepdims=True)
        actives.append(active)
        d_uppers.append(d_upper.astype(LOW))
    active = jnp.concatenate(actives, axis=1)
    d_upper = jnp.concatenate(d_uppers, axis=1)
    mixed_ref[...] += dot(active, w_ref[1])
    da_ref[...] += dot(d_upper, w_ref[0])
    rows = dw_ref.shape[2]
    dw_ref[:, 0] = dot(d_upper, a_second, TN).astype(LOW).reshape(-1, rows, dw_ref.shape[3])
    dw_ref[:, 1] = dot(active, dy, TN).astype(LOW).reshape(-1, rows, dw_ref.shape[3])

    @pl.when(pl.program_id(0) == pl.num_programs(0) - 1)
    def _():
        out_ref[...] = (resid_ref[...] + mixed_ref[...] + rows_ref[3:4]).astype(LOW)
        d_resid, d_gain, d_bias = norm_back(
            normed_ref[...], rstd_ref[...], rows_ref[1:2], da_ref[...]
        )
        dy_wide = dy_ref[...].astype(WIDE)
        d_resid += dy_wide
        resid_ref[...] = d_resid
        sums_ref[0:1] = d_gain[None]
        sums_ref[1:2] = d_bias[None]
        sums_ref[2:3] = jnp.sum(d_resid, axis=0, keepdims=True)
        sums_ref[3:4] = jnp.sum(dy_wide, axis=0, keepdims=True)
        sums_ref[4:8] = jnp.zeros_like(sums_ref[4:8])
        low = d_resid.astype(LOW)
        split = mine_ref.shape[0]
        mine_ref[...] = dot(w_out_ref[:split], low, NT).astype(LOW)
        theirs_ref[...] = dot(w_out_ref[split:], low, NT).astype(LOW)
        dw_out_ref[...] = dot(attn_ref[...], low).astype(LOW)


def middle_call(attn, w_out, x, dy, rows, weights, bias, parts):
    tokens, width = x.shape
    hidden = weights.shape[1]
    once = pl.Buffered(1)

    def whole(*shape):
        return pl.BlockSpec(shape, lambda g: (0,) * len(shape), pipeline_mode=once)

    some = pl.BlockSpec((2, UNITS, width), lambda g: (0, g, 0))
    each = hidden // parts
    slots = pl.BlockSpec((UNITS // each, 2, each, width), lambda g: (g, 0, 0, 0))
    row = pl.BlockSpec((1, UNITS), lambda g: (0, g))
    local = attn.shape[0] // 2
    return pl.pallas_call(
        middle,
        grid=(hidden // UNITS,),
        in_specs=[
            whole(*attn.shape),
            whole(*w_out.shape),
            whole(tokens, width),
            whole(tokens, width),
            whole(*rows.shape),
            some,
            row,
        ],
        out_specs=[
            whole(tokens, width),
            whole(local, tokens),
            whole(local, tokens),
            whole(tokens, width),
            whole(*w_out.shape),
            whole(8, width),
            slots,
            row,
        ],
        out_shape=[
            jax.ShapeDtypeStruct((tokens, width), LOW),
            jax.ShapeDtypeStruct((local, tokens), LOW),
            jax.ShapeDtypeStruct((local, tokens), LOW),
            jax.ShapeDtypeStruct((tokens, width), WIDE),
            jax.ShapeDtypeStruct(w_out.shape, LOW),
            jax.ShapeDtypeStruct((8, width), WIDE),
            jax.ShapeDtypeStruct((parts, 2, each, width), LOW),
            jax.ShapeDtypeStruct((1, hidden), WIDE),
        ],
        scratch_shapes=[
            pltpu.VMEM((tokens, width), LOW),
            pltpu.VMEM((tokens, width), WIDE),
            pltpu.VMEM((tokens, 1), WIDE),
            pltpu.VMEM((tokens, width), WIDE),
            pltpu.VMEM((tokens, width), WIDE),
        ],
        compiler_params=pltpu.CompilerParams(vmem_limit_bytes=56 * 2**20),
        cost_estimate=SMALL,
        name="middle",
    )(attn, w_out, x, dy, rows, weights, bias)


def first_back(half_ref, d_a_ref, d_b_ref, w_a_ref, w_b_ref, *refs):
    mine_ref, theirs_ref = refs[-2:]
    own = mine_ref.shape[0]
    for out_ref, which in ((theirs_ref, 1 - half_ref[0]), (mine_ref, half_ref[0])):
        some = pl.ds(pl.multiple_of(which * own, own), own)
        value = dot(d_a_ref[:, some], w_a_ref[...], TN) + dot(d_b_ref[:, some], w_b_ref[...], TN)
        out_ref[...] = value.astype(out_ref.dtype)


def first_back_call(half, d_a, d_b, w_a, w_b, own, *earlier):
    width = w_a.shape[1]

    def whole(*shape):
        return pl.BlockSpec(shape, lambda g, h: (0,) * len(shape))

    return pl.pallas_call(
        first_back,
        grid_spec=pltpu.PrefetchScalarGridSpec(
            num_scalar_prefetch=1,
            grid=(1,),
            in_specs=[whole(*v.shape) for v in (d_a, d_b, w_a, w_b)] + [ANY] * len(earlier),
            out_specs=[whole(own, width), whole(own, width)],
        ),
        out_shape=[
            jax.ShapeDtypeStruct((own, width), WIDE),
            jax.ShapeDtypeStruct((own, width), LOW),
        ],
        compiler_params=pltpu.CompilerParams(vmem_limit_bytes=VMEM),
        cost_estimate=SMALL,
        name="first_back",
    )(half[None], d_a, d_b, w_a, w_b, *earlier)


def weight_back(place_ref, a_ref, d_a_ref, d_b_ref, *refs):
    refs[-1][0, 0] = dot(d_a_ref[0], a_ref[...]).astype(LOW)
    refs[-1][0, 1] = dot(d_b_ref[0], a_ref[...]).astype(LOW)


def weight_back_call(place, a_first, d_a, d_b, *earlier):
    count, rows, tokens = d_a.shape
    width = a_first.shape[1]
    piece = pl.BlockSpec((1, rows, tokens), lambda k, p: (index_of(k, p[0], count), 0, 0))
    return pl.pallas_call(
        weight_back,
        grid_spec=pltpu.PrefetchScalarGridSpec(
            num_scalar_prefetch=1,
            grid=(count,),
            in_specs=[pl.BlockSpec((tokens, width), lambda k, p: (0, 0)), piece, piece]
            + [ANY] * len(earlier),
            out_specs=pl.BlockSpec((1, 2, rows, width), lambda k, p: (k, 0, 0, 0)),
        ),
        out_shape=jax.ShapeDtypeStruct((count, 2, rows, width), LOW),
        compiler_params=pltpu.CompilerParams(vmem_limit_bytes=VMEM),
        cost_estimate=SMALL,
        name="weight_back",
    )(place[None], a_first, d_a, d_b, *earlier)


def shards(
    inputs,
    gain1,
    bias1,
    w_qkv,
    bias_q,
    bias_v,
    w_out,
    bias_out,
    gain2,
    bias2,
    w_fc,
    bias_fc,
    w_proj,
    bias_proj,
    cotangent,
):
    n_dp, n_t = lax.axis_size("dp"), lax.axis_size("tensor")
    place, me = lax.axis_index("dp"), lax.axis_index("tensor")
    count, width = inputs.shape
    local = w_qkv.shape[2]
    hidden = w_fc.shape[1]
    heads = local // HEAD
    scale = HEAD ** (-0.5)
    own = count // n_t
    half = lax.rem(me, 2)
    rows_q, rows_o, rows_f = 3 * local // n_dp, local // n_dp, hidden // n_dp

    plane = exchanges(n_dp)
    near, last = plane[:-1], plane[-1]

    qkv_own = w_qkv.transpose(1, 2, 0).reshape(3 * local, width)
    q = across(lax.dynamic_slice_in_dim(qkv_own, place * rows_q, rows_q, 0), 2, n_t)
    vector = across(jnp.concatenate([bias_q, bias_v, bias_fc]), 2, n_t)
    biases = [bias_fc, vector[2 * local :], across(bias_fc, 1, n_t), across(bias_fc, 3, n_t)]
    o = lax.dynamic_slice_in_dim(w_out, place * rows_o, rows_o, 0)
    o_parts = to_others(o, n_t)
    w = jnp.stack(
        [
            lax.dynamic_slice_in_dim(w_fc, place * rows_f, rows_f, 1).T,
            lax.dynamic_slice_in_dim(w_proj, place * rows_f, rows_f, 0),
        ]
    )
    w = lax.all_gather(w, ("dp", "tensor"), axis=1, tiled=True)

    x_seq = lax.dynamic_slice_in_dim(inputs, (me // 2) * LEN, LEN, 0).astype(WIDE)
    normed, _ = norm_parts(x_seq)
    a_first = (normed * gain1 + bias1).astype(LOW)

    def project(weight, add_q, add_v):
        proj = dot(weight, a_first, NT)
        query = (proj[:local] + add_q[:, None]) * scale
        values = proj[2 * local :] + add_v[:, None]
        proj = jnp.concatenate([query, proj[local : 2 * local], values], axis=0)
        return proj.astype(LOW).reshape(3, heads, HEAD, LEN)

    def halves(value):
        mine = lax.dynamic_slice_in_dim(value, half * own, own, value.ndim - 1)
        theirs = lax.dynamic_slice_in_dim(value, (1 - half) * own, own, value.ndim - 1)
        return mine, theirs

    def both(held, step, axis=0):
        return jnp.concatenate([held, swap(held, step)], axis=axis)

    q, o = q[None], jnp.stack([o] + o_parts)[None]
    for step in near:
        q = both(q, step)
    q_take = swap(q, last)
    proj_a = project(qkv_own, bias_q, bias_v)
    out_a, lse_a = attention(proj_a)
    mine_a, theirs_a = halves(out_a.reshape(local, LEN))
    theirs_a = across(theirs_a, 1, n_t)
    for step in plane:
        o = both(o, step)
    qkv_other = by_index(jnp.concatenate([q, q_take], axis=0), place, LOW)
    qkv_other = qkv_other.reshape(3 * local, width)
    proj_b = project(qkv_other, vector[:local], vector[local : 2 * local])
    out_b, lse_b = attention(proj_b)
    mine_b, theirs_b = halves(out_b.reshape(local, LEN))
    theirs_b = across(theirs_b, 1, n_t)
    w_out_all = groups_by_index(o, place).reshape(n_t * local, width)
    attn_low = jnp.concatenate([mine_a, mine_b, theirs_a, theirs_b], axis=0)
    place_of = jnp.array([ORDER.index(m) for m in range(n_t)], jnp.int32)
    place_of = place_of[jnp.arange(n_t, dtype=jnp.int32) ^ me]
    bias_fc_all = jnp.stack(biases).reshape(n_t, n_dp, rows_f)
    bias_fc_all = bias_fc_all.at[place_of].get(mode="promise_in_bounds")
    bias_fc_all = bias_fc_all.transpose(1, 0, 2).reshape(1, n_t * hidden)

    x_own = lax.dynamic_slice_in_dim(inputs, me * own, own, 0)
    dy = lax.dynamic_slice_in_dim(cotangent, me * own, own, 0)
    rows = jnp.stack([bias_out, gain2, bias2, bias_proj])
    output, d_mine, d_theirs, d_resid, o, sums_row, w, sums_fc = middle_call(
        attn_low, w_out_all, x_own, dy, rows, w, bias_fc_all, n_dp
    )
    from_left = to_right(output, n_t)
    d_take = across(d_theirs, 1, n_t)
    output_near = (from_left, to_left(after(output, d_take), n_t))

    def parted(held, axis=0):
        middle = held.shape[axis] // 2
        return jnp.split(held, [middle], axis=axis)

    def folded(held, taken, axis=0):
        held, taken = parted(held, axis), parted(taken, axis)
        return add_low(held[0], taken[0]), add_low(held[1], taken[1])

    w = lax.psum_scatter(w, "dp")
    d_out = jnp.where(
        half == 0,
        jnp.concatenate([d_mine, d_take], axis=1),
        jnp.concatenate([d_take, d_mine], axis=1),
    )
    d_out = d_out.reshape(2, heads, HEAD, LEN)

    down = near[::-1]
    d_proj_a = attention_back(proj_a, out_a, d_out[0], lse_a)
    d_proj_b = attention_back(proj_b, out_b, d_out[1], lse_b, d_proj_a)
    d_proj_a = d_proj_a.reshape(3 * local, LEN)
    d_proj_b = d_proj_b.reshape(3 * local, LEN)

    d_first, d_theirs = first_back_call(
        half, d_proj_a, d_proj_b, qkv_own, qkv_other, own
    )
    d_first_take = across(d_theirs, 1, n_t)
    output_near = tuple(after(part, d_first_take) for part in output_near)
    output_far = onward(output_near, n_t)
    sums_a = jnp.sum(d_proj_a.reshape(3, local, LEN).astype(WIDE), axis=2)
    sums_b = jnp.sum(d_proj_b.reshape(3, local, LEN).astype(WIDE), axis=2)
    group = jnp.arange(n_t, dtype=jnp.int32)[None, :, None]
    bias_rows = jnp.where(group == me, sums_a[:, None], 0.0)
    bias_rows += jnp.where(group == (me ^ 2), sums_b[:, None], 0.0)
    sums_fc = after(sums_fc, d_first_take).reshape(n_dp, n_t, rows_f).transpose(1, 0, 2)
    w = w.reshape(2, n_t, rows_f, width)
    w = [lax.dynamic_index_in_dim(w, me ^ m, 1, keepdims=False) for m in ORDER]
    w_parts = [across(w[at], m, n_t) for at, m in enumerate(ORDER) if at]
    normed1, rstd1 = norm_parts(x_own.astype(WIDE))
    d_first = d_first + d_first_take.astype(WIDE)
    d_in_norm, d_gain1, d_bias1 = norm_back(normed1, rstd1, after(gain1, *output_near), d_first)
    d_inputs = (d_resid + d_in_norm).astype(LOW)
    inputs_near = to_right(d_inputs, n_t), to_left(d_inputs, n_t)

    d_proj_a, d_proj_b = (d.reshape(n_dp, rows_q, LEN) for d in (d_proj_a, d_proj_b))
    q, q_send = parted(weight_back_call(place, a_first, d_proj_a, d_proj_b, d_inputs))
    q_take = swap(q_send, last)
    o, o_send = parted(groups_by_slot(o.reshape(n_t, n_dp, rows_o, width), place, d_inputs))
    o_take = swap(o_send, last)
    for step in down:
        q, q_send = folded(q, q_take)
        q_take = swap(q_send, step)
        o, o_send = folded(o, o_take)
        o_take = swap(o_send, step)

    def sum_tensor(held):
        return held[0], [across(held[at], m, n_t) for at, m in enumerate(ORDER) if at]

    def total_of(mine, parts):
        total = mine.astype(WIDE)
        for part in parts:
            total += part.astype(WIDE)
        return total.astype(LOW)

    w_parts[0] = after(w_parts[0], *output_far, *inputs_near)
    w = total_of(w[0], w_parts)[:, None]
    inputs_far = onward(inputs_near, n_t)
    o, o_parts = sum_tensor(add_low(o, after(o_take, w))[0])
    q = add_low(q, after(q_take, w))[0]
    q_take = across(q[1], 2, n_t)
    vectors = jnp.concatenate(
        [
            d_gain1,
            d_bias1,
            sums_row[:4].reshape(-1),
            bias_rows[0].reshape(-1),
            bias_rows[2].reshape(-1),
            sums_fc.reshape(-1),
        ]
    ).reshape(-1, 128)
    vectors = after(vectors, d_inputs)
    for step in plane:
        vectors = vectors + swap(vectors, step)
    vectors = after(vectors, w)
    vectors = vectors + across(vectors, 1, n_t)
    vectors = after(vectors, *inputs_far)
    vectors = vectors + across(vectors, 2, n_t)
    o = total_of(o, o_parts)[None]
    q = add_low(q[0], q_take)[None]
    for step in plane:
        o, q = both(o, step), both(q, step)
    for step in plane:
        w = both(w, step, 1)
    d_w_out = by_index(o, place, WIDE).reshape(local, width)
    d_w_qkv = by_index(q, place, WIDE).reshape(3, local, width).transpose(2, 0, 1)
    whole_output = assembled(output, output_near, output_far)
    whole_d_inputs = assembled(d_inputs, inputs_near, inputs_far)
    d_w_fc, d_w_proj = turned_by_index(w, place)
    vectors = vectors.reshape(-1, width)
    d_gain1, d_bias1, d_gain2, d_bias2, d_bias_out, d_bias_proj = (vectors[r] for r in range(6))
    d_bias_q = lax.dynamic_slice_in_dim(vectors[6], me * local, local, 0)
    d_bias_v = lax.dynamic_slice_in_dim(vectors[7], me * local, local, 0)
    d_bias_fc = lax.dynamic_slice_in_dim(vectors[8:].reshape(-1), me * hidden, hidden, 0)
    return (
        whole_output,
        whole_d_inputs,
        d_gain1,
        d_bias1,
        d_w_qkv,
        d_bias_q,
        d_bias_v,
        d_w_out,
        d_bias_out,
        d_gain2,
        d_bias2,
        d_w_fc,
        d_bias_fc,
        d_w_proj,
        d_bias_proj,
    )


def solution(mesh):
    placed = (
        P("dp", None),
        P(),
        P(),
        P(None, None, "tensor"),
        P("tensor"),
        P("tensor"),
        P("tensor", None),
        P(),
        P(),
        P(),
        P(None, "tensor"),
        P("tensor"),
        P("tensor", None),
        P(),
        P("dp", None),
    )
    return jax.shard_map(
        shards,
        mesh=mesh,
        in_specs=placed,
        out_specs=(
            P("dp", None),
            P("dp", None),
            P(),
            P(),
            P(None, None, "tensor"),
            P("tensor"),
            P("tensor"),
            P("tensor", None),
            P(),
            P(),
            P(),
            P(None, "tensor"),
            P("tensor"),
            P("tensor", None),
            P(),
        ),
        check_vma=False,
    )
```

```python
import jax
import jax.numpy as jnp
from jax import lax
from jax.experimental import pallas as pl
from jax.experimental.pallas import tpu as pltpu
from jax.sharding import PartitionSpec as P

HEAD = 64
LEN = 1024
BLOCK = 256
UNITS = 768
VMEM = 32 * 2**20
SMALL = pl.CostEstimate(flops=1, bytes_accessed=1, transcendentals=0)


LOW = jnp.bfloat16
WIDE = jnp.float32

NN = (((1,), (0,)), ((), ()))
NT = (((1,), (1,)), ((), ()))
TN = (((0,), (0,)), ((), ()))
TT = (((0,), (1,)), ((), ()))


def dot(left, right, dims=NN):
    return lax.dot_general(left, right, dims, preferred_element_type=WIDE)


def norm_parts(value):
    centre = value - jnp.mean(value, axis=-1, keepdims=True)
    rstd = lax.rsqrt(jnp.mean(centre * centre, axis=-1, keepdims=True) + 1e-05)
    return (centre * rstd, rstd)


def norm_back(normed, rstd, gain, grad):
    scaled = grad * gain
    inner = (
        scaled
        - jnp.mean(scaled, axis=-1, keepdims=True)
        - normed * jnp.mean(scaled * normed, axis=-1, keepdims=True)
    )
    return (rstd * inner, jnp.sum(grad * normed, axis=0), jnp.sum(grad, axis=0))


def causal(scores):
    keys = lax.broadcasted_iota(jnp.int32, scores.shape, 0)
    queries = lax.broadcasted_iota(jnp.int32, scores.shape, 1)
    return keys <= queries


def attend(q_ref, k_ref, v_ref, o_ref, lse_ref):
    query, values = q_ref[0, 0], v_ref[0, 0]
    keys = k_ref[0, 0].T
    for lo in range(0, LEN, BLOCK):
        hi = lo + BLOCK
        near = dot(keys[lo:hi], query[:, lo:hi])
        near = jnp.where(causal(near), near, -1e30)
        top = jnp.max(near, axis=0, keepdims=True)
        if lo:
            far = dot(keys[:lo], query[:, lo:hi])
            top = jnp.maximum(top, jnp.max(far, axis=0, keepdims=True))
        near = jnp.exp(near - top)
        total = jnp.sum(near, axis=0, keepdims=True)
        out = dot(values[:, lo:hi], near.astype(LOW))
        if lo:
            far = jnp.exp(far - top)
            total += jnp.sum(far, axis=0, keepdims=True)
            out += dot(values[:, :lo], far.astype(LOW))
        o_ref[0, :, lo:hi] = (out / total).astype(LOW)
        lse_ref[0, :, lo:hi] = top + jnp.log(total)


def attend_back(q_ref, k_ref, v_ref, o_ref, do_ref, lse_ref, *refs):
    out_ref, dq_ref = refs[-2:]
    query, keys_t, d_out = q_ref[0, 0], k_ref[0, 0], do_ref[0]
    keys, values = keys_t.T, v_ref[0, 0].T
    lse = lse_ref[0]
    delta = jnp.sum(d_out.astype(WIDE) * o_ref[0].astype(WIDE), axis=0, keepdims=True)

    def part(lo, hi, begin, end, mask):
        probs = jnp.exp(dot(keys[lo:hi], query[:, begin:end]) - lse[:, begin:end])
        if mask:
            probs = jnp.where(causal(probs), probs, 0.0)
        d_probs = dot(values[lo:hi], d_out[:, begin:end])
        d_scores = (probs * (d_probs - delta[:, begin:end])).astype(LOW)
        d_values = dot(d_out[:, begin:end], probs.astype(LOW), NT)
        d_keys = dot(query[:, begin:end], d_scores, NT)
        d_query = dot(keys_t[:, lo:hi], d_scores)
        if lo == 0:
            dq_ref[:, begin:end] = d_query
        else:
            dq_ref[:, begin:end] += d_query
        return d_keys, d_values

    for lo in range(0, LEN, BLOCK):
        hi = lo + BLOCK
        d_keys, d_values = part(lo, hi, lo, hi, True)
        if hi < LEN:
            more_keys, more_values = part(lo, hi, hi, LEN, False)
            d_keys += more_keys
            d_values += more_values
        out_ref[1, 0, :, lo:hi] = d_keys.astype(LOW)
        out_ref[2, 0, :, lo:hi] = d_values.astype(LOW)
    d_query = dq_ref[...].astype(LOW).astype(WIDE) * HEAD ** (-0.5)
    out_ref[0, 0] = d_query.astype(LOW)


ANY = pl.BlockSpec(memory_space=pl.ANY)


def kind(which):
    return pl.BlockSpec((1, 1, HEAD, LEN), lambda head: (which, head, 0, 0))


QKV = [kind(0), kind(1), kind(2)]
PER_HEAD = pl.BlockSpec((1, HEAD, LEN), lambda head: (head, 0, 0))
PER_ROW = pl.BlockSpec((1, 1, LEN), lambda head: (head, 0, 0))


def attention(qkv):
    heads = qkv.shape[1]
    return pl.pallas_call(
        attend,
        grid=(heads,),
        in_specs=QKV,
        out_specs=[PER_HEAD, PER_ROW],
        out_shape=[
            jax.ShapeDtypeStruct((heads, HEAD, LEN), LOW),
            jax.ShapeDtypeStruct((heads, 1, LEN), WIDE),
        ],
        compiler_params=pltpu.CompilerParams(vmem_limit_bytes=VMEM),
        cost_estimate=SMALL,
        name="attention",
    )(qkv, qkv, qkv)


def attention_back(qkv, out, d_out, lse, *earlier):
    heads = qkv.shape[1]
    return pl.pallas_call(
        attend_back,
        grid=(heads,),
        in_specs=QKV + [PER_HEAD, PER_HEAD, PER_ROW] + [ANY] * len(earlier),
        out_specs=pl.BlockSpec((3, 1, HEAD, LEN), lambda head: (0, head, 0, 0)),
        out_shape=jax.ShapeDtypeStruct((3, heads, HEAD, LEN), LOW),
        scratch_shapes=[pltpu.VMEM((HEAD, LEN), WIDE)],
        compiler_params=pltpu.CompilerParams(vmem_limit_bytes=VMEM),
        cost_estimate=SMALL,
        name="attention_back",
    )(qkv, qkv, qkv, out, d_out, lse, *earlier)


def bits(size, odd):
    above = [1 << b for b in range(1, size.bit_length() - 1)]
    return above if odd else above[::-1]


def exchanges(size):
    steps = [
        [(d, d ^ (odd if d & 1 else even)) for d in range(size)]
        for even, odd in zip(bits(size, False), bits(size, True))
    ]
    return steps + [[(d, d ^ 1) for d in range(size)]]


def turned(value, size, odd):
    count = size.bit_length() - 2
    back = value * 0
    for b in range(count):
        back = back | (((value >> b) & 1) << (count - 1 - b))
    return jnp.where(odd == 1, value, back)


def slot_of(index, place, size):
    mask = index ^ place
    low = mask & 1
    return low * (size // 2) + turned(mask >> 1, size, (place & 1) ^ low)


def index_of(slot, place, size):
    low = slot // (size // 2)
    return ((turned(slot % (size // 2), size, (place & 1) ^ low) << 1) | low) ^ place


def swap(value, step):
    return lax.ppermute(value, "dp", step)


def add_low(left, right):
    return (left.astype(WIDE) + right.astype(WIDE)).astype(LOW)


def across(piece, mask, size):
    return lax.ppermute(piece, "tensor", [(t, t ^ mask) for t in range(size)])


ORDER = (0, 2, 1, 3)


def to_others(piece, size):
    return [across(piece, m, size) for m in ORDER[1:]]


def nothing(*refs):
    pass


def after(value, *earlier):
    return pl.pallas_call(
        nothing,
        in_specs=[ANY] * (1 + len(earlier)),
        out_specs=ANY,
        out_shape=jax.ShapeDtypeStruct(value.shape, value.dtype),
        input_output_aliases={0: 0},
        cost_estimate=SMALL,
        name="after",
    )(value, *earlier)


def to_right(piece, size):
    return lax.ppermute(piece, "tensor", [(t, (t + 1) % size) for t in range(size)])


def to_left(piece, size):
    return lax.ppermute(piece, "tensor", [(t, (t - 1) % size) for t in range(size)])


def onward(pair, size):
    rows = pair[0].shape[0] // 2
    return to_right(pair[0][:rows], size), to_left(pair[1][rows:], size)


def assemble_near(me_ref, own_ref, left_ref, right_ref, out_ref):
    for step, piece_ref in enumerate((own_ref, left_ref, right_ref)):

        @pl.when(pl.program_id(0) == step)
        def _(piece_ref=piece_ref):
            out_ref[...] = piece_ref[...]


def assemble_far(me_ref, whole_ref, first_ref, second_ref, out_ref):
    rows = first_ref.shape[0]
    out_ref[:rows] = first_ref[...]
    out_ref[rows:] = second_ref[...]


def assembled(own, near, far):
    size = 4
    rows, width = own.shape
    full = pl.BlockSpec((rows, width), lambda g, me: (0, 0))
    part = pl.BlockSpec((rows // 2, width), lambda g, me: (0, 0))

    def turn(g):
        return jnp.where(g == 2, 1, -g)

    shape = jax.ShapeDtypeStruct((size * rows, width), own.dtype)
    me = lax.axis_index("tensor")[None]
    whole = pl.pallas_call(
        assemble_near,
        grid_spec=pltpu.PrefetchScalarGridSpec(
            num_scalar_prefetch=1,
            grid=(3,),
            in_specs=[full, full, full],
            out_specs=pl.BlockSpec(
                (rows, width), lambda g, me: (lax.rem(me[0] + turn(g) + size, size), 0)
            ),
        ),
        out_shape=shape,
        compiler_params=pltpu.CompilerParams(vmem_limit_bytes=VMEM),
        cost_estimate=SMALL,
        name="assemble_near",
    )(me, own, *near)
    return pl.pallas_call(
        assemble_far,
        grid_spec=pltpu.PrefetchScalarGridSpec(
            num_scalar_prefetch=1,
            grid=(1,),
            in_specs=[ANY, part, part],
            out_specs=pl.BlockSpec((rows, width), lambda g, me: (lax.rem(me[0] + 2, size), 0)),
        ),
        out_shape=shape,
        input_output_aliases={1: 0},
        compiler_params=pltpu.CompilerParams(vmem_limit_bytes=VMEM),
        cost_estimate=SMALL,
        name="assemble_far",
    )(me, whole, *far)


def pick(place_ref, in_ref, *refs):
    refs[-1][...] = in_ref[...].reshape(refs[-1].shape).astype(refs[-1].dtype)


def reorder_call(kernel, place, values, earlier, count, in_spec, out_spec, shape, dtype):
    return pl.pallas_call(
        kernel,
        grid_spec=pltpu.PrefetchScalarGridSpec(
            num_scalar_prefetch=1,
            grid=(count,),
            in_specs=[in_spec] * len(values) + [ANY] * len(earlier),
            out_specs=out_spec,
        ),
        out_shape=jax.ShapeDtypeStruct(shape, dtype),
        compiler_params=pltpu.CompilerParams(vmem_limit_bytes=VMEM),
        name="reorder",
    )(place[None], *values, *earlier)


def by_index(slots, place, dtype, *earlier):
    count, rows, width = slots.shape
    return reorder_call(
        pick,
        place,
        [slots],
        earlier,
        count,
        pl.BlockSpec((1, rows, width), lambda j, p: (slot_of(j, p[0], count), 0, 0)),
        pl.BlockSpec((1, rows, width), lambda j, p: (j, 0, 0)),
        slots.shape,
        dtype,
    )


def split_two(place_ref, in_ref, first_ref, second_ref):
    first_ref[0] = in_ref[0, 0].astype(first_ref.dtype)
    second_ref[0] = in_ref[1, 0].astype(second_ref.dtype)


def two_by_index(slots, place):
    _, count, rows, width = slots.shape
    one = pl.BlockSpec((1, rows, width), lambda j, p: (j, 0, 0))
    shape = (count, rows, width)
    return pl.pallas_call(
        split_two,
        grid_spec=pltpu.PrefetchScalarGridSpec(
            num_scalar_prefetch=1,
            grid=(count,),
            in_specs=[
                pl.BlockSpec((2, 1, rows, width), lambda j, p: (0, slot_of(j, p[0], count), 0, 0))
            ],
            out_specs=[one, one],
        ),
        out_shape=[jax.ShapeDtypeStruct(shape, LOW), jax.ShapeDtypeStruct(shape, WIDE)],
        compiler_params=pltpu.CompilerParams(vmem_limit_bytes=VMEM),
        name="reorder",
    )(place[None], slots)


def turn_two(place_ref, *refs):
    first_ref, second_ref = refs[-2:]
    pieces = [ref[:, 0].astype(WIDE) for ref in refs[:-2]]
    first_ref[...] = jnp.concatenate([piece[0] for piece in pieces], axis=0).T
    second_ref[...] = jnp.concatenate([piece[1] for piece in pieces], axis=0)


def turned_by_index(slots, place):
    _, count, rows, width = slots.shape
    if 4 * rows % 128:
        first, second = two_by_index(slots, place)
        first = first.reshape(count * rows, width).T.astype(WIDE)
        return first, second.reshape(count * rows, width)

    def piece(at):
        return pl.BlockSpec(
            (2, 1, rows, width), lambda g, p: (0, slot_of(4 * g + at, p[0], count), 0, 0)
        )

    return pl.pallas_call(
        turn_two,
        grid_spec=pltpu.PrefetchScalarGridSpec(
            num_scalar_prefetch=1,
            grid=(count // 4,),
            in_specs=[piece(at) for at in range(4)],
            out_specs=[
                pl.BlockSpec((width, 4 * rows), lambda g, p: (0, g)),
                pl.BlockSpec((4 * rows, width), lambda g, p: (g, 0)),
            ],
        ),
        out_shape=[
            jax.ShapeDtypeStruct((width, count * rows), WIDE),
            jax.ShapeDtypeStruct((count * rows, width), WIDE),
        ],
        compiler_params=pltpu.CompilerParams(vmem_limit_bytes=VMEM),
        cost_estimate=SMALL,
        name="reorder",
    )(place[None], slots, slots, slots, slots)


def groups_by_index(slots, place):
    count, groups, rows, width = slots.shape
    return reorder_call(
        pick,
        place,
        [slots],
        (),
        count,
        pl.BlockSpec((1, groups, rows, width), lambda j, p: (slot_of(j, p[0], count), 0, 0, 0)),
        pl.BlockSpec((groups, 1, rows, width), lambda j, p: (0, j, 0, 0)),
        (groups, count, rows, width),
        LOW,
    )


def groups_by_slot(values, place, *earlier):
    groups, count, rows, width = values.shape
    return reorder_call(
        pick,
        place,
        [values],
        earlier,
        count,
        pl.BlockSpec((groups, 1, rows, width), lambda k, p: (0, index_of(k, p[0], count), 0, 0)),
        pl.BlockSpec((1, groups, rows, width), lambda k, p: (k, 0, 0, 0)),
        (count, groups, rows, width),
        LOW,
    )


def middle(
    attn_ref, w_out_ref, x_ref, dy_ref, rows_ref, w_ref, bias_ref,
    out_ref, mine_ref, theirs_ref, resid_ref, dw_out_ref, sums_ref, dw_ref, db_ref,
    a_ref, normed_ref, rstd_ref, mixed_ref, da_ref,
):
    @pl.when(pl.program_id(0) == 0)
    def _():
        resid = x_ref[...].astype(WIDE) + dot(attn_ref[...], w_out_ref[...], TN) + rows_ref[0:1]
        normed, rstd = norm_parts(resid)
        resid_ref[...] = resid
        normed_ref[...] = normed
        rstd_ref[...] = rstd
        a_ref[...] = (normed * rows_ref[1:2] + rows_ref[2:3]).astype(LOW)
        mixed_ref[...] = jnp.zeros_like(mixed_ref)
        da_ref[...] = jnp.zeros_like(da_ref)

    a_second, dy = a_ref[...], dy_ref[...]
    actives, d_uppers = [], []
    for lo in range(0, UNITS, BLOCK):
        some = slice(lo, lo + BLOCK)
        upper = dot(a_second, w_ref[0, some], NT) + bias_ref[:, some]
        square = upper * upper
        curve = jnp.tanh(0.7978845608028654 * (upper + 0.044715 * upper * square))
        rise = 0.5 * (1.0 + curve)
        active = (upper * rise).astype(LOW)
        slope = rise + 0.5 * upper * (1.0 - curve * curve) * (
            0.7978845608028654 * (1.0 + 3.0 * 0.044715 * square)
        )
        d_upper = dot(dy, w_ref[1, some], NT) * slope
        db_ref[:, some] = jnp.sum(d_upper, axis=0, keepdims=True)
        actives.append(active)
        d_uppers.append(d_upper.astype(LOW))
    active = jnp.concatenate(actives, axis=1)
    d_upper = jnp.concatenate(d_uppers, axis=1)
    mixed_ref[...] += dot(active, w_ref[1])
    da_ref[...] += dot(d_upper, w_ref[0])
    rows = dw_ref.shape[2]
    dw_ref[:, 0] = dot(d_upper, a_second, TN).astype(LOW).reshape(-1, rows, dw_ref.shape[3])
    dw_ref[:, 1] = dot(active, dy, TN).astype(LOW).reshape(-1, rows, dw_ref.shape[3])

    @pl.when(pl.program_id(0) == pl.num_programs(0) - 1)
    def _():
        out_ref[...] = (resid_ref[...] + mixed_ref[...] + rows_ref[3:4]).astype(LOW)
        d_resid, d_gain, d_bias = norm_back(
            normed_ref[...], rstd_ref[...], rows_ref[1:2], da_ref[...]
        )
        dy_wide = dy_ref[...].astype(WIDE)
        d_resid += dy_wide
        resid_ref[...] = d_resid
        sums_ref[0:1] = d_gain[None]
        sums_ref[1:2] = d_bias[None]
        sums_ref[2:3] = jnp.sum(d_resid, axis=0, keepdims=True)
        sums_ref[3:4] = jnp.sum(dy_wide, axis=0, keepdims=True)
        sums_ref[4:8] = jnp.zeros_like(sums_ref[4:8])
        low = d_resid.astype(LOW)
        split = mine_ref.shape[0]
        mine_ref[...] = dot(w_out_ref[:split], low, NT).astype(LOW)
        theirs_ref[...] = dot(w_out_ref[split:], low, NT).astype(LOW)
        dw_out_ref[...] = dot(attn_ref[...], low).astype(LOW)


def middle_call(attn, w_out, x, dy, rows, weights, bias, parts):
    tokens, width = x.shape
    hidden = weights.shape[1]
    once = pl.Buffered(1)

    def whole(*shape):
        return pl.BlockSpec(shape, lambda g: (0,) * len(shape), pipeline_mode=once)

    some = pl.BlockSpec((2, UNITS, width), lambda g: (0, g, 0))
    each = hidden // parts
    slots = pl.BlockSpec((UNITS // each, 2, each, width), lambda g: (g, 0, 0, 0))
    row = pl.BlockSpec((1, UNITS), lambda g: (0, g))
    local = attn.shape[0] // 2
    return pl.pallas_call(
        middle,
        grid=(hidden // UNITS,),
        in_specs=[
            whole(*attn.shape),
            whole(*w_out.shape),
            whole(tokens, width),
            whole(tokens, width),
            whole(*rows.shape),
            some,
            row,
        ],
        out_specs=[
            whole(tokens, width),
            whole(local, tokens),
            whole(local, tokens),
            whole(tokens, width),
            whole(*w_out.shape),
            whole(8, width),
            slots,
            row,
        ],
        out_shape=[
            jax.ShapeDtypeStruct((tokens, width), LOW),
            jax.ShapeDtypeStruct((local, tokens), LOW),
            jax.ShapeDtypeStruct((local, tokens), LOW),
            jax.ShapeDtypeStruct((tokens, width), WIDE),
            jax.ShapeDtypeStruct(w_out.shape, LOW),
            jax.ShapeDtypeStruct((8, width), WIDE),
            jax.ShapeDtypeStruct((parts, 2, each, width), LOW),
            jax.ShapeDtypeStruct((1, hidden), WIDE),
        ],
        scratch_shapes=[
            pltpu.VMEM((tokens, width), LOW),
            pltpu.VMEM((tokens, width), WIDE),
            pltpu.VMEM((tokens, 1), WIDE),
            pltpu.VMEM((tokens, width), WIDE),
            pltpu.VMEM((tokens, width), WIDE),
        ],
        compiler_params=pltpu.CompilerParams(vmem_limit_bytes=56 * 2**20),
        cost_estimate=SMALL,
        name="middle",
    )(attn, w_out, x, dy, rows, weights, bias)


def first_back(half_ref, d_a_ref, d_b_ref, w_a_ref, w_b_ref, *refs):
    mine_ref, theirs_ref = refs[-2:]
    own = mine_ref.shape[0]
    for out_ref, which in ((theirs_ref, 1 - half_ref[0]), (mine_ref, half_ref[0])):
        some = pl.ds(pl.multiple_of(which * own, own), own)
        value = dot(d_a_ref[:, some], w_a_ref[...], TN) + dot(d_b_ref[:, some], w_b_ref[...], TN)
        out_ref[...] = value.astype(out_ref.dtype)


def first_back_call(half, d_a, d_b, w_a, w_b, own, *earlier):
    width = w_a.shape[1]

    def whole(*shape):
        return pl.BlockSpec(shape, lambda g, h: (0,) * len(shape))

    return pl.pallas_call(
        first_back,
        grid_spec=pltpu.PrefetchScalarGridSpec(
            num_scalar_prefetch=1,
            grid=(1,),
            in_specs=[whole(*v.shape) for v in (d_a, d_b, w_a, w_b)] + [ANY] * len(earlier),
            out_specs=[whole(own, width), whole(own, width)],
        ),
        out_shape=[
            jax.ShapeDtypeStruct((own, width), WIDE),
            jax.ShapeDtypeStruct((own, width), LOW),
        ],
        compiler_params=pltpu.CompilerParams(vmem_limit_bytes=VMEM),
        cost_estimate=SMALL,
        name="first_back",
    )(half[None], d_a, d_b, w_a, w_b, *earlier)


def weight_back(place_ref, a_ref, d_a_ref, d_b_ref, *refs):
    refs[-1][0, 0] = dot(d_a_ref[0], a_ref[...]).astype(LOW)
    refs[-1][0, 1] = dot(d_b_ref[0], a_ref[...]).astype(LOW)


def weight_back_call(place, a_first, d_a, d_b, *earlier):
    count, rows, tokens = d_a.shape
    width = a_first.shape[1]
    piece = pl.BlockSpec((1, rows, tokens), lambda k, p: (index_of(k, p[0], count), 0, 0))
    return pl.pallas_call(
        weight_back,
        grid_spec=pltpu.PrefetchScalarGridSpec(
            num_scalar_prefetch=1,
            grid=(count,),
            in_specs=[pl.BlockSpec((tokens, width), lambda k, p: (0, 0)), piece, piece]
            + [ANY] * len(earlier),
            out_specs=pl.BlockSpec((1, 2, rows, width), lambda k, p: (k, 0, 0, 0)),
        ),
        out_shape=jax.ShapeDtypeStruct((count, 2, rows, width), LOW),
        compiler_params=pltpu.CompilerParams(vmem_limit_bytes=VMEM),
        cost_estimate=SMALL,
        name="weight_back",
    )(place[None], a_first, d_a, d_b, *earlier)


def shards(
    inputs,
    gain1,
    bias1,
    w_qkv,
    bias_q,
    bias_v,
    w_out,
    bias_out,
    gain2,
    bias2,
    w_fc,
    bias_fc,
    w_proj,
    bias_proj,
    cotangent,
):
    n_dp, n_t = lax.axis_size("dp"), lax.axis_size("tensor")
    place, me = lax.axis_index("dp"), lax.axis_index("tensor")
    count, width = inputs.shape
    local = w_qkv.shape[2]
    hidden = w_fc.shape[1]
    heads = local // HEAD
    scale = HEAD ** (-0.5)
    own = count // n_t
    half = lax.rem(me, 2)
    rows_q, rows_o, rows_f = 3 * local // n_dp, local // n_dp, hidden // n_dp

    plane = exchanges(n_dp)
    near, last = plane[:-1], plane[-1]

    qkv_own = w_qkv.transpose(1, 2, 0).reshape(3 * local, width)
    q = across(lax.dynamic_slice_in_dim(qkv_own, place * rows_q, rows_q, 0), 2, n_t)
    vector = across(jnp.concatenate([bias_q, bias_v, bias_fc]), 2, n_t)
    biases = [bias_fc, vector[2 * local :], across(bias_fc, 1, n_t), across(bias_fc, 3, n_t)]
    o = lax.dynamic_slice_in_dim(w_out, place * rows_o, rows_o, 0)
    o_parts = to_others(o, n_t)
    w = jnp.stack(
        [
            lax.dynamic_slice_in_dim(w_fc, place * rows_f, rows_f, 1).T,
            lax.dynamic_slice_in_dim(w_proj, place * rows_f, rows_f, 0),
        ]
    )
    w = lax.all_gather(w, ("dp", "tensor"), axis=1, tiled=True)

    x_seq = lax.dynamic_slice_in_dim(inputs, (me // 2) * LEN, LEN, 0).astype(WIDE)
    normed, _ = norm_parts(x_seq)
    a_first = (normed * gain1 + bias1).astype(LOW)

    def project(weight, add_q, add_v):
        proj = dot(weight, a_first, NT)
        query = (proj[:local] + add_q[:, None]) * scale
        values = proj[2 * local :] + add_v[:, None]
        proj = jnp.concatenate([query, proj[local : 2 * local], values], axis=0)
        return proj.astype(LOW).reshape(3, heads, HEAD, LEN)

    def halves(value):
        mine = lax.dynamic_slice_in_dim(value, half * own, own, value.ndim - 1)
        theirs = lax.dynamic_slice_in_dim(value, (1 - half) * own, own, value.ndim - 1)
        return mine, theirs

    def both(held, step, axis=0):
        return jnp.concatenate([held, swap(held, step)], axis=axis)

    q, o = q[None], jnp.stack([o] + o_parts)[None]
    for step in near:
        q = both(q, step)
    q_take = swap(q, last)
    proj_a = project(qkv_own, bias_q, bias_v)
    out_a, lse_a = attention(proj_a)
    mine_a, theirs_a = halves(out_a.reshape(local, LEN))
    theirs_a = across(theirs_a, 1, n_t)
    for step in plane:
        o = both(o, step)
    qkv_other = by_index(jnp.concatenate([q, q_take], axis=0), place, LOW)
    qkv_other = qkv_other.reshape(3 * local, width)
    proj_b = project(qkv_other, vector[:local], vector[local : 2 * local])
    out_b, lse_b = attention(proj_b)
    mine_b, theirs_b = halves(out_b.reshape(local, LEN))
    theirs_b = across(theirs_b, 1, n_t)
    w_out_all = groups_by_index(o, place).reshape(n_t * local, width)
    attn_low = jnp.concatenate([mine_a, mine_b, theirs_a, theirs_b], axis=0)
    place_of = jnp.array([ORDER.index(m) for m in range(n_t)], jnp.int32)
    place_of = place_of[jnp.arange(n_t, dtype=jnp.int32) ^ me]
    bias_fc_all = jnp.stack(biases).reshape(n_t, n_dp, rows_f)
    bias_fc_all = bias_fc_all.at[place_of].get(mode="promise_in_bounds")
    bias_fc_all = bias_fc_all.transpose(1, 0, 2).reshape(1, n_t * hidden)

    x_own = lax.dynamic_slice_in_dim(inputs, me * own, own, 0)
    dy = lax.dynamic_slice_in_dim(cotangent, me * own, own, 0)
    rows = jnp.stack([bias_out, gain2, bias2, bias_proj])
    output, d_mine, d_theirs, d_resid, o, sums_row, w, sums_fc = middle_call(
        attn_low, w_out_all, x_own, dy, rows, w, bias_fc_all, n_dp
    )
    from_left = to_right(output, n_t)
    d_take = across(d_theirs, 1, n_t)
    output_near = (from_left, to_left(after(output, d_take), n_t))

    def parted(held, axis=0):
        middle = held.shape[axis] // 2
        return jnp.split(held, [middle], axis=axis)

    def folded(held, taken, axis=0):
        held, taken = parted(held, axis), parted(taken, axis)
        return add_low(held[0], taken[0]), add_low(held[1], taken[1])

    w = lax.psum_scatter(w, "dp")
    d_out = jnp.where(
        half == 0,
        jnp.concatenate([d_mine, d_take], axis=1),
        jnp.concatenate([d_take, d_mine], axis=1),
    )
    d_out = d_out.reshape(2, heads, HEAD, LEN)

    down = near[::-1]
    d_proj_a = attention_back(proj_a, out_a, d_out[0], lse_a)
    d_proj_b = attention_back(proj_b, out_b, d_out[1], lse_b, d_proj_a)
    d_proj_a = d_proj_a.reshape(3 * local, LEN)
    d_proj_b = d_proj_b.reshape(3 * local, LEN)

    d_first, d_theirs = first_back_call(
        half, d_proj_a, d_proj_b, qkv_own, qkv_other, own
    )
    d_first_take = across(d_theirs, 1, n_t)
    output_near = tuple(after(part, d_first_take) for part in output_near)
    output_far = onward(output_near, n_t)
    sums_a = jnp.sum(d_proj_a.reshape(3, local, LEN).astype(WIDE), axis=2)
    sums_b = jnp.sum(d_proj_b.reshape(3, local, LEN).astype(WIDE), axis=2)
    group = jnp.arange(n_t, dtype=jnp.int32)[None, :, None]
    bias_rows = jnp.where(group == me, sums_a[:, None], 0.0)
    bias_rows += jnp.where(group == (me ^ 2), sums_b[:, None], 0.0)
    sums_fc = after(sums_fc, d_first_take).reshape(n_dp, n_t, rows_f).transpose(1, 0, 2)
    w = w.reshape(2, n_t, rows_f, width)
    w = [lax.dynamic_index_in_dim(w, me ^ m, 1, keepdims=False) for m in ORDER]
    w_parts = [across(w[at], m, n_t) for at, m in enumerate(ORDER) if at]
    normed1, rstd1 = norm_parts(x_own.astype(WIDE))
    d_first = d_first + d_first_take.astype(WIDE)
    d_in_norm, d_gain1, d_bias1 = norm_back(normed1, rstd1, after(gain1, *output_near), d_first)
    d_inputs = (d_resid + d_in_norm).astype(LOW)
    inputs_near = to_right(d_inputs, n_t), to_left(d_inputs, n_t)

    d_proj_a, d_proj_b = (d.reshape(n_dp, rows_q, LEN) for d in (d_proj_a, d_proj_b))
    q, q_send = parted(weight_back_call(place, a_first, d_proj_a, d_proj_b, d_inputs))
    q_take = swap(q_send, last)
    o, o_send = parted(groups_by_slot(o.reshape(n_t, n_dp, rows_o, width), place, d_inputs))
    o_take = swap(o_send, last)
    for step in down:
        q, q_send = folded(q, q_take)
        q_take = swap(q_send, step)
        o, o_send = folded(o, o_take)
        o_take = swap(o_send, step)

    def sum_tensor(held):
        return held[0], [across(held[at], m, n_t) for at, m in enumerate(ORDER) if at]

    def total_of(mine, parts):
        total = mine.astype(WIDE)
        for part in parts:
            total += part.astype(WIDE)
        return total.astype(LOW)

    w_parts[0] = after(w_parts[0], *output_far, *inputs_near)
    w = total_of(w[0], w_parts)[:, None]
    inputs_far = onward(inputs_near, n_t)
    o, o_parts = sum_tensor(add_low(o, after(o_take, w))[0])
    q = add_low(q, after(q_take, w))[0]
    q_take = across(q[1], 2, n_t)
    vectors = jnp.concatenate(
        [
            d_gain1,
            d_bias1,
            sums_row[:4].reshape(-1),
            bias_rows[0].reshape(-1),
            bias_rows[2].reshape(-1),
            sums_fc.reshape(-1),
        ]
    ).reshape(-1, 128)
    vectors = after(vectors, d_inputs)
    for step in plane:
        vectors = vectors + swap(vectors, step)
    vectors = after(vectors, w)
    vectors = vectors + across(vectors, 1, n_t)
    vectors = vectors + across(vectors, 2, n_t)
    o = total_of(o, o_parts)[None]
    q = add_low(q[0], q_take)[None]
    for step in plane:
        o, q = both(o, step), both(q, step)
    for step in plane:
        w = both(w, step, 1)
    d_w_out = by_index(o, place, WIDE).reshape(local, width)
    d_w_qkv = by_index(q, place, WIDE).reshape(3, local, width).transpose(2, 0, 1)
    whole_output = assembled(output, output_near, output_far)
    whole_d_inputs = assembled(d_inputs, inputs_near, inputs_far)
    d_w_fc, d_w_proj = turned_by_index(w, place)
    vectors = vectors.reshape(-1, width)
    d_gain1, d_bias1, d_gain2, d_bias2, d_bias_out, d_bias_proj = (vectors[r] for r in range(6))
    d_bias_q = lax.dynamic_slice_in_dim(vectors[6], me * local, local, 0)
    d_bias_v = lax.dynamic_slice_in_dim(vectors[7], me * local, local, 0)
    d_bias_fc = lax.dynamic_slice_in_dim(vectors[8:].reshape(-1), me * hidden, hidden, 0)
    return (
        whole_output,
        whole_d_inputs,
        d_gain1,
        d_bias1,
        d_w_qkv,
        d_bias_q,
        d_bias_v,
        d_w_out,
        d_bias_out,
        d_gain2,
        d_bias2,
        d_w_fc,
        d_bias_fc,
        d_w_proj,
        d_bias_proj,
    )


def solution(mesh):
    placed = (
        P("dp", None),
        P(),
        P(),
        P(None, None, "tensor"),
        P("tensor"),
        P("tensor"),
        P("tensor", None),
        P(),
        P(),
        P(),
        P(None, "tensor"),
        P("tensor"),
        P("tensor", None),
        P(),
        P("dp", None),
    )
    return jax.shard_map(
        shards,
        mesh=mesh,
        in_specs=placed,
        out_specs=(
            P("dp", None),
            P("dp", None),
            P(),
            P(),
            P(None, None, "tensor"),
            P("tensor"),
            P("tensor"),
            P("tensor", None),
            P(),
            P(),
            P(),
            P(None, "tensor"),
            P("tensor"),
            P("tensor", None),
            P(),
        ),
        check_vma=False,
    )
```
